128 devices in a mesh: dp: 4 (over x), fsdp: 32 (over z, y, core).
Axes of the slice: x: 4, y: 4, z: 4, core: 2. Of those that a mesh axis runs over, the one named last changes fastest.
Arguments:
- features: bfloat16 [98304, 512], P(('dp', 'fsdp')), may hold values from -1200 to 1200
- bn_gain: float32 [512], replicated, may hold values from 0.5 to 1.5
- bn_bias: float32 [512], replicated, may hold values from -3 to 3
- gate_weights: bfloat16 [6, 1024, 1536], P(None, 'fsdp'), may hold values from -0.1875 to 0.1875
- feature_masks: int32 [6, 512], replicated, may hold values 0 or 1
- head_first: bfloat16 [512, 256], P('fsdp'), may hold values from -0.25 to 0.25
- head_first_bias: float32 [256], replicated, may hold values from -3 to 3
- head_second: bfloat16 [256, 10], P('fsdp'), may hold values from -0.75 to 0.75
- head_second_bias: float32 [10], replicated, may hold values from -3 to 3
- labels: int32 [98304], P(('dp', 'fsdp')), may hold values from 0 to 9
Outputs:
- features_grad: float32 [98304, 512], P(('dp', 'fsdp'))
- bn_gain_grad: float32 [512], replicated
- bn_bias_grad: float32 [512], replicated
- gate_weights_grad: float32 [6, 1024, 1536], P(None, 'fsdp')
- head_first_grad: float32 [512, 256], P('fsdp')
- head_first_bias_grad: float32 [256], replicated
- head_second_grad: float32 [256, 10], P('fsdp')
- head_second_bias_grad: float32 [10], replicated
The draws below stay inside these ranges and needn't reach their ends.
All inputs are finite; a program needn't handle non-finite values.
Results may differ from the reference program's by a relative error of at most 0.0095.
Values may be sent and summed in bfloat16 or wider, within the bound.
No kernel may reach another device: no remote copies, remote signals or barrier semaphores. Data moves between devices by JAX's collectives and lax.ppermute only.
A program may use at most 192 MiB of HBM per device.

```python
import math
import jax
import jax.numpy as jnp
from jax import lax

F = 512
HID = 256
CLASSES = 10
SECTIONS = 6
ROWS_DEV = 768
ROWS = 98304


def draw_features(key, part):
    key = jax.random.fold_in(key, 11)
    noise_key, scale_key, mean_key, row_key = jax.random.split(key, 4)
    position = jnp.arange(ROWS, dtype=jnp.float32) / max(ROWS - 1, 1)
    column_scale = jnp.exp(jax.random.uniform(scale_key, (F,), jnp.float32, 0.0, math.log(10.0)))
    noise = jnp.clip(jax.random.normal(noise_key, (ROWS, F), jnp.float32), -6.0, 6.0)
    column_mean = column_scale * jax.random.uniform(mean_key, (F,), jnp.float32, -1.5, 1.5)
    trend = jnp.exp(position * math.log(3.0))
    row_scale = trend * jnp.exp(jax.random.uniform(row_key, (ROWS,), jnp.float32, 0.0, math.log(3.5)))
    return ((column_mean[None, :] + column_scale[None, :] * noise) * row_scale[:, None]).astype(jnp.bfloat16)


def plant(entries, own_key, smallest, largest):
    shape = entries.shape
    index_at = [jax.random.randint(jax.random.fold_in(own_key, axis), (), 0, shape[axis]) for axis in range(len(shape))]
    entries = entries.at[tuple(index_at)].set(smallest)
    longest = shape.index(max(shape))
    index_at[longest] = (index_at[longest] + 1) % shape[longest]
    return entries.at[tuple(index_at)].set(largest)


def level_of(stream_key, dims, pieces, smallest, top_value):
    factor_of, own = 1.0, jax.random.fold_in(stream_key, 6)
    for axis_at, parts in pieces:
        draws = jnp.exp(jax.random.uniform(jax.random.fold_in(own, axis_at), (parts,), jnp.float32, smallest / len(pieces), top_value / len(pieces)))
        factor_of = factor_of * jnp.repeat(draws, dims[axis_at] // parts).reshape([-1 if axis == axis_at else 1 for axis in range(len(dims))])
    return factor_of


def centred(own_key, shape, deviation, most, cuts=(), kind=jnp.bfloat16):
    drawn = jax.random.normal(own_key, shape, jnp.float32) * deviation
    if len(cuts) > 0:
        drawn = level_of(own_key, shape, cuts, -0.22, 0.18) * drawn
    return jnp.clip(drawn, min=-most, max=most).astype(kind)


def setup_inputs(seed: int = 0) -> dict:
    seeds = jax.random.split(jax.random.key(seed), 11)
    return {
        "features": draw_features(jax.random.fold_in(seeds[10], 71), 0),
        "bn_gain": jnp.clip(1.0 + 0.1 * jax.random.normal(seeds[1], (F,), jnp.float32), 0.5, 1.5),
        "bn_bias": centred(seeds[2], (F,), 0.5, 3.0, (), jnp.float32),
        "gate_weights": centred(seeds[3], (SECTIONS, 2 * F, 3 * F), (2 * F) ** -0.5, 0.1875, ((1, 32),)),
        "feature_masks": plant((jax.random.randint(seeds[4], (SECTIONS, F), 0, 2) < 1).astype(jnp.int32), jax.random.fold_in(seeds[4], 1), 0, 1),
        "head_first": centred(seeds[5], (F, HID), F ** -0.5, 0.25, ((0, 32),)),
        "head_first_bias": centred(seeds[6], (HID,), 0.5, 3.0, (), jnp.float32),
        "head_second": centred(seeds[7], (HID, CLASSES), (HID // 4) ** -0.5, 0.75, ((0, 32),)),
        "head_second_bias": centred(seeds[8], (CLASSES,), 0.5, 3.0, (), jnp.float32),
        "labels": plant(jax.random.randint(seeds[9], (ROWS,), 0, CLASSES), jax.random.fold_in(seeds[9], 1), 0, CLASSES - 1).astype(jnp.int32),
    }


@jax.custom_vjp
def low(v):
    return lax.optimization_barrier(v.astype(jnp.bfloat16)).astype(jnp.float32)

@jax.custom_vjp
def low_back(v):
    return v

def low_keep(v):
    return (low(v), None)

def low_pass(kept, grad):
    return (grad,)

def back_keep(v):
    return (v, None)

def back_low(kept, grad):
    return (low(grad),)
low.defvjp(low_keep, low_pass)
low_back.defvjp(back_keep, back_low)
epsilon = 1e-05

def product(left, right):
    return jnp.dot(left, right, preferred_element_type=jnp.float32, precision=lax.Precision.HIGHEST)

def exact_gelu(value):
    return jax.nn.gelu(value, approximate=False)

def gflu_section(hidden_state, masked_low, weight):
    joined = jnp.concatenate([low(hidden_state), masked_low], 1)
    gate_pair = low_back(product(joined, weight[:, :2 * F]))
    update = jax.nn.sigmoid(gate_pair[:, :F])
    reset_gate = jax.nn.sigmoid(gate_pair[:, F:])
    second = jnp.concatenate([low(reset_gate * hidden_state), masked_low], 1)
    output = jnp.tanh(low_back(product(second, weight[:, 2 * F:])))
    return hidden_state + update * (output - hidden_state)

def forward(inputs, gain, bias, gate_float, first, first_bias, second, second_bias, mask_rows, labels):
    feature_mean = lax.optimization_barrier(jnp.mean(inputs, 0))
    variance = lax.optimization_barrier(jnp.mean(inputs * inputs, 0)) - feature_mean * feature_mean
    normed = (inputs - feature_mean) * lax.rsqrt(variance + epsilon)
    scaled = normed * gain + bias
    block = math.gcd(ROWS, 4096)

    def block_loss(total, item):
        rows_in, block_labels = item
        hidden_state = rows_in
        for layer_index in range(SECTIONS):
            hidden_state = gflu_section(hidden_state, low(rows_in * mask_rows[layer_index]), gate_float[layer_index])
        head_in = low(hidden_state)
        pre_first = low_back(product(head_in, first) + first_bias)
        activation = low(exact_gelu(pre_first))
        logits = low_back(product(activation, second) + second_bias)
        hits = block_labels[:, None] == jnp.arange(CLASSES, dtype=jnp.int32)[None, :]
        picked = lax.optimization_barrier(jnp.sum(jnp.where(hits, logits, jnp.zeros_like(logits)), 1))
        return (total + jnp.sum(jax.nn.logsumexp(logits, 1) - picked), None)
    total, ignored = lax.scan(jax.checkpoint(block_loss), jnp.zeros((), jnp.float32), (scaled.reshape(ROWS // block, block, F), labels.reshape(ROWS // block, block)))
    return total / ROWS_DEV

def reference(features, bn_gain, bn_bias, gate_weights, feature_masks, head_first, head_first_bias, head_second, head_second_bias, labels):
    mask_rows = feature_masks.astype(jnp.float32)

    def loss_of(inputs, gain, bias, gate_float, first, first_bias, second, second_bias):
        return forward(inputs, gain, bias, gate_float, first, first_bias, second, second_bias, mask_rows, labels)
    loss_value, pullback = jax.vjp(loss_of, features.astype(jnp.float32), bn_gain, bn_bias, gate_weights.astype(jnp.float32), head_first.astype(jnp.float32), head_first_bias, head_second.astype(jnp.float32), head_second_bias)
    grads = pullback(jnp.ones((), jnp.float32))
    return (grads[0], grads[1], grads[2], grads[3], grads[4], grads[5], grads[6], grads[7])
```

```python
import functools
import math

import jax
import jax.numpy as jnp
import numpy as np
from jax import lax
from jax.experimental import pallas as pl
from jax.experimental.pallas import tpu as pltpu
from jax.sharding import PartitionSpec as P

epsilon = 1e-05
F32 = jnp.float32
BF16 = jnp.bfloat16
VMEM_LIMIT = 60 * 1024 * 1024
GROUPS = ((5, 4, 3), (2, 1, 0))
HEAD_ROWS = 16
LANES = 128


def sigmoid(value):
    return 0.5 * jnp.tanh(0.5 * value) + 0.5


def dot(left, right):
    return jnp.dot(left, right, preferred_element_type=F32)


def dot_cols(left, right):
    return lax.dot_general(left, right, (((1,), (1,)), ((), ())), preferred_element_type=F32)


def erf(value):
    value = jnp.clip(value, -4.0, 4.0)
    square = value * value
    top = jnp.full_like(square, -2.72614225801306e-10)
    for term in (
        2.77068142495902e-08,
        -2.10102402082508e-06,
        -5.69250639462346e-05,
        -7.34990630326855e-04,
        -2.95459980854025e-03,
        -1.60960333262415e-02,
    ):
        top = top * square + term
    low = jnp.full_like(square, -1.45660718464996e-05)
    for term in (
        -2.13374055278905e-04,
        -1.68282697438203e-03,
        -7.37332916720468e-03,
        -1.42647390514189e-02,
    ):
        low = low * square + term
    return value * top / low


def normalise(total_rows, features, stats):
    mean = stats[0:1] / total_rows
    scale = lax.rsqrt(stats[1:2] / total_rows - mean * mean + epsilon)
    return (features.astype(F32) - mean) * scale, scale


def halves(rows):
    return [slice(0, rows // 2), slice(rows // 2, rows)]


def forward_kernel(
    total_rows, x_ref, stat_ref, gain_ref, bias_ref, mask_ref, w_ref,
    s_ref, u_ref, r_ref, o_ref, last_ref, turned_ref, low_ref, state_ref,
):
    n = pl.program_id(0)
    rows, width = x_ref.shape
    half = w_ref.shape[0] // 2

    @pl.when(n == 0)
    def _():
        for part in halves(rows):
            normed, _ = normalise(total_rows, x_ref[part], stat_ref[...])
            scaled = normed * gain_ref[...] + bias_ref[...]
            state_ref[part] = scaled
            low = scaled.astype(BF16)
            low_ref[part] = low
            turned_ref[:, part] = low.T

    mask = mask_ref[0].astype(BF16)

    def weight(lower, start):
        at = w_ref[0:half, :, start : start + width] if lower else w_ref[half:, :, start : start + width]
        return at.reshape(width, width)

    for part in halves(rows):
        state = state_ref[part]
        state_low = state.astype(BF16)
        masked = low_ref[part] * mask
        s_ref[0, part] = state
        reset = sigmoid(dot(state_low, weight(True, width)) + dot(masked, weight(False, width)))
        r_ref[0, part] = reset
        second = (reset * state).astype(BF16)
        update = sigmoid(dot(state_low, weight(True, 0)) + dot(masked, weight(False, 0)))
        u_ref[0, part] = update
        output = jnp.tanh(
            dot(second, weight(True, 2 * width)) + dot(masked, weight(False, 2 * width))
        )
        o_ref[0, part] = output
        state_ref[part] = state + update * (output - state)

    @pl.when(n == pl.num_programs(0) - 1)
    def _():
        last_ref[...] = state_ref[...]


def run_forward(features, stats, gain, bias, masks, weights, total_rows):
    rows, width = features.shape
    sections = masks.shape[0]
    owners = weights.shape[0]
    depth = 2 * width // owners
    whole = lambda n: (0, 0)
    saved = jax.ShapeDtypeStruct((sections, rows, width), F32)
    saved_spec = pl.BlockSpec((1, rows, width), lambda n: (n, 0, 0))
    return pl.pallas_call(
        functools.partial(forward_kernel, total_rows),
        grid=(sections,),
        in_specs=[
            pl.BlockSpec((rows, width), whole),
            pl.BlockSpec((2, width), whole),
            pl.BlockSpec((1, width), whole),
            pl.BlockSpec((1, width), whole),
            pl.BlockSpec((1, 1, width), lambda n: (n, 0, 0)),
            pl.BlockSpec((owners, depth, 3 * width), lambda n: (0, n, 0)),
        ],
        out_specs=[saved_spec] * 4
        + [pl.BlockSpec((rows, width), whole), pl.BlockSpec((width, rows), whole)],
        out_shape=[saved] * 4
        + [jax.ShapeDtypeStruct((rows, width), F32), jax.ShapeDtypeStruct((width, rows), BF16)],
        scratch_shapes=[pltpu.VMEM((rows, width), BF16), pltpu.VMEM((rows, width), F32)],
        compiler_params=pltpu.CompilerParams(vmem_limit_bytes=VMEM_LIMIT),
        name="sections_forward",
    )(features, stats, gain, bias, masks, weights)


def head_kernel(
    row_scale, classes, state_ref, w_ref, b1_ref, b2_ref, label_ref,
    grad_ref, share_ref, sum1_ref, sum2_ref,
):
    rows, width = state_ref.shape
    owners = w_ref.shape[0]
    hidden = b1_ref.shape[1]
    first = w_ref[:, :, 0:hidden].reshape(width, hidden)
    second = w_ref[:, :, hidden : hidden + LANES].astype(F32)[:, 0 : hidden // owners]
    second = second.reshape(hidden, LANES).astype(BF16)
    head_in = state_ref[...].astype(BF16)
    pre = dot(head_in, first) + b1_ref[...]
    phi = 0.5 + 0.5 * erf(pre * math.sqrt(0.5))
    activation = (pre * phi).astype(BF16)
    slope = phi + pre * (jnp.exp(-0.5 * pre * pre) * (1.0 / math.sqrt(2.0 * math.pi)))
    lane = lax.broadcasted_iota(jnp.int32, (rows, LANES), 1)
    logits = dot(activation, second) + b2_ref[...]
    logits = jnp.where(lane < classes, logits, -1e30)
    powers = jnp.exp(logits - jnp.max(logits, 1, keepdims=True))
    chance = powers / jnp.sum(powers, 1, keepdims=True)
    hit = jnp.where(lane == label_ref[...], 1.0, 0.0)
    grad_logits = ((chance - hit) * row_scale).astype(BF16)
    sum2_ref[...] = jnp.sum(grad_logits.astype(F32), 0, keepdims=True)
    grad_second = dot(activation.T, grad_logits)
    grad_pre = (dot_cols(grad_logits, second) * slope).astype(BF16)
    sum1_ref[...] = jnp.sum(grad_pre.astype(F32), 0, keepdims=True)
    grad_first = dot(head_in.T, grad_pre)
    grad_ref[...] = dot_cols(grad_pre, first)
    grad_second = grad_second.reshape(owners, hidden // owners, LANES)
    grad_second = jnp.concatenate([grad_second, jnp.zeros_like(grad_second)], 1)
    share_ref[:, :, 0:hidden] = grad_first.reshape(owners, HEAD_ROWS, hidden).astype(BF16)
    share_ref[:, :, hidden : hidden + LANES] = grad_second.astype(BF16)
    tail = share_ref.shape[2] - hidden - LANES
    share_ref[:, :, hidden + LANES :] = jnp.zeros((owners, HEAD_ROWS, tail), BF16)


def run_head(state, weights, block_at, b1, b2, labels, classes):
    rows, width = state.shape
    owners, _, columns = weights.shape
    hidden = b1.shape[1]
    taken = hidden + LANES
    whole = lambda i: (0, 0)
    return pl.pallas_call(
        functools.partial(head_kernel, 1.0 / rows, classes),
        grid=(1,),
        in_specs=[
            pl.BlockSpec((rows, width), whole),
            pl.BlockSpec((owners, HEAD_ROWS, taken), lambda i: (0, block_at, 0)),
            pl.BlockSpec((1, hidden), whole),
            pl.BlockSpec((1, LANES), whole),
            pl.BlockSpec((rows, 1), whole),
        ],
        out_specs=[
            pl.BlockSpec((rows, width), whole),
            pl.BlockSpec((owners, HEAD_ROWS, columns), lambda i: (0, 0, 0)),
            pl.BlockSpec((1, hidden), whole),
            pl.BlockSpec((1, LANES), whole),
        ],
        out_shape=[
            jax.ShapeDtypeStruct((rows, width), F32),
            jax.ShapeDtypeStruct((owners, HEAD_ROWS, columns), BF16),
            jax.ShapeDtypeStruct((1, hidden), F32),
            jax.ShapeDtypeStruct((1, LANES), F32),
        ],
        compiler_params=pltpu.CompilerParams(vmem_limit_bytes=VMEM_LIMIT),
        name="head",
    )(state, weights, b1, b2, labels)


def backward_kernel(
    total_rows, opening, closing, *refs
):
    refs = list(refs)
    s_ref, u_ref, r_ref, o_ref, w_ref, turned_ref, row_ref, column_ref, g_ref = refs[:9]
    refs = refs[9:]
    if opening:
        share_ref = refs.pop(0)
    else:
        gs_ref = refs.pop(0)
    if closing:
        x_ref, stat_ref = refs.pop(0), refs.pop(0)
    dw_ref, gout_ref, gsout_ref = refs.pop(0), refs.pop(0), refs.pop(0)
    if closing:
        sums_ref = refs.pop(0)
    made_ref, left_ref, grads_ref, dw_sem, share_sem = refs
    step = pl.program_id(0)
    steps = pl.num_programs(0)
    rows, width = g_ref.shape
    owners, depth = w_ref.shape[0], w_ref.shape[1]
    half = owners // 2

    def share_copy():
        return pltpu.make_async_copy(
            share_ref, dw_ref.at[:, pl.ds(dw_ref.shape[1] - HEAD_ROWS, HEAD_ROWS), :], share_sem
        )

    def dw_copy(at, slot):
        return pltpu.make_async_copy(
            made_ref.at[slot],
            dw_ref.at[:, pl.ds(pl.multiple_of(at * depth, depth), depth), :],
            dw_sem.at[slot],
        )

    slot = lax.rem(step, 2)

    @pl.when(step == 0)
    def _():
        if opening:
            share_copy().start()
            gsout_ref[...] = jnp.zeros_like(gsout_ref)
        else:
            gsout_ref[...] = gs_ref[...]
        gout_ref[...] = g_ref[...]

    def weight(lower, start, count):
        at = w_ref[0:half, :, start : start + count] if lower else w_ref[half:, :, start : start + count]
        return at.reshape(width, count)

    for part in halves(rows):
        grad = gout_ref[part]
        state, update, reset, output = s_ref[0, part], u_ref[0, part], r_ref[0, part], o_ref[0, part]
        left_ref[0, :, part] = state.astype(BF16).T
        left_ref[1, :, part] = (reset * state).astype(BF16).T
        grad_out = (grad * update * (1.0 - output * output)).astype(BF16)
        grads_ref[part, 2 * width :] = grad_out
        through = dot_cols(grad_out, weight(True, 2 * width, width))
        grad_update = (grad * (output - state) * update * (1.0 - update)).astype(BF16)
        grads_ref[part, 0:width] = grad_update
        grad_reset = (through * state * reset * (1.0 - reset)).astype(BF16)
        grads_ref[part, width : 2 * width] = grad_reset
        gout_ref[part] = (
            grad * (1.0 - update)
            + through * reset
            + dot_cols(grad_update, weight(True, 0, width))
            + dot_cols(grad_reset, weight(True, width, width))
        )
        gsout_ref[part] += row_ref[0] * (
            dot_cols(grad_update, weight(False, 0, width))
            + dot_cols(grad_reset, weight(False, width, width))
            + dot_cols(grad_out, weight(False, 2 * width, width))
        )

    @pl.when(step >= 2)
    def _():
        dw_copy(step - 2, slot).wait()

    for at in range(3):
        columns = slice(at * width, (at + 1) * width)
        made = dot(left_ref[at // 2], grads_ref[:, columns])
        made_ref[slot, 0:half, :, columns] = made.astype(BF16).reshape(half, depth, width)
        made = column_ref[0] * dot(turned_ref[...], grads_ref[:, columns])
        made_ref[slot, half:, :, columns] = made.astype(BF16).reshape(half, depth, width)
    dw_copy(step, slot).start()

    @pl.when(step == steps - 1)
    def _():
        dw_copy(step, slot).wait()

        @pl.when(steps > 1)
        def _():
            dw_copy(step - 1, 1 - slot).wait()

        if opening:
            share_copy().wait()
        if closing:
            total = gsout_ref[...] + gout_ref[...]
            gsout_ref[...] = total
            normed, _ = normalise(total_rows, x_ref[...], stat_ref[...])
            sums_ref[0:1] = jnp.sum(total, 0, keepdims=True)
            sums_ref[1:2] = jnp.sum(total * normed, 0, keepdims=True)


def run_backward(
    group, saved, weights, turned, masks, grad_state, grad_scaled, share, features, stats, total_rows
):
    opening, closing = share is not None, features is not None
    top, count = group[0], len(group)
    rows, width = grad_state.shape
    owners = weights.shape[0]
    depth = 2 * width // owners
    whole = lambda i: (0, 0)
    section = lambda i: (top - i, 0, 0)
    saved_spec = pl.BlockSpec((1, rows, width), section)
    tall_spec = pl.BlockSpec((rows, width), whole)
    in_specs = [saved_spec] * 4 + [
        pl.BlockSpec((owners, depth, 3 * width), lambda i: (0, top - i, 0)),
        pl.BlockSpec((width, rows), whole),
        pl.BlockSpec((1, 1, width), section),
        pl.BlockSpec((1, width, 1), section),
        tall_spec,
    ]
    operands = [*saved, weights, turned, masks, masks.reshape(-1, width, 1), grad_state]
    if opening:
        in_specs.append(pl.BlockSpec(share.shape, lambda i: (0, 0, 0)))
        operands.append(share)
    else:
        in_specs.append(tall_spec)
        operands.append(grad_scaled)
    if closing:
        in_specs += [tall_spec, pl.BlockSpec((2, width), whole)]
        operands += [features, stats]
    out_specs = [pl.BlockSpec(memory_space=pl.ANY), tall_spec, tall_spec]
    made_rows = count * depth + (HEAD_ROWS if opening else 0)
    out_shape = [
        jax.ShapeDtypeStruct((owners, made_rows, 3 * width), BF16),
        jax.ShapeDtypeStruct((rows, width), F32),
        jax.ShapeDtypeStruct((rows, width), F32),
    ]
    if closing:
        out_specs.append(pl.BlockSpec((2, width), whole))
        out_shape.append(jax.ShapeDtypeStruct((2, width), F32))
    return pl.pallas_call(
        functools.partial(backward_kernel, total_rows, opening, closing),
        grid=(count,),
        in_specs=in_specs,
        out_specs=out_specs,
        out_shape=out_shape,
        scratch_shapes=[
            pltpu.VMEM((2, owners, depth, 3 * width), BF16),
            pltpu.VMEM((2, width, rows), BF16),
            pltpu.VMEM((rows, 3 * width), BF16),
            pltpu.SemaphoreType.DMA((2,)),
            pltpu.SemaphoreType.DMA,
        ],
        compiler_params=pltpu.CompilerParams(vmem_limit_bytes=VMEM_LIMIT),
        name="sections_backward",
    )(*operands)


def pairs(sizes, axis, flip):
    table = []
    for source in range(math.prod(sizes)):
        place = list(np.unravel_index(source, sizes))
        place[axis] ^= flip
        table.append((source, int(np.ravel_multi_index(place, sizes))))
    return table


def everywhere_sum(value, sizes, names):
    for axis in reversed(range(len(sizes))):
        for flip in (1, 3) if sizes[axis] == 4 else (1,):
            value = value + lax.ppermute(value, names, pairs(sizes, axis, flip))
    return value


def on_device(
    sizes,
    features,
    bn_gain,
    bn_bias,
    gate_weights,
    feature_masks,
    head_first,
    head_first_bias,
    head_second,
    head_second_bias,
    labels,
):
    names = ("dp", "fsdp")
    rows, width = features.shape
    sections, depth, columns = gate_weights.shape
    hidden = head_first.shape[1]
    classes = head_second.shape[1]
    total_rows = rows * math.prod(sizes)
    gain, bias = bn_gain[None], bn_bias[None]
    masks = feature_masks.astype(F32)[:, None, :]
    b1 = head_first_bias[None]
    b2 = jnp.pad(head_second_bias, (0, LANES - classes))[None]

    inputs = features.astype(F32)
    stats = jnp.stack([jnp.sum(inputs, 0), jnp.sum(inputs * inputs, 0)])
    stats = everywhere_sum(stats.reshape(-1, LANES), sizes, names).reshape(2, width)

    extra = jnp.pad(head_first, ((0, 0), (0, columns - hidden))) + jnp.pad(
        head_second, ((0, HEAD_ROWS - head_second.shape[0]), (hidden, columns - hidden - classes))
    )
    shard = jnp.concatenate([gate_weights.reshape(sections * depth, columns), extra], 0)
    weights = lax.all_gather(shard, "fsdp", axis=0)

    *saved, state, turned = run_forward(features, stats, gain, bias, masks, weights, total_rows)
    grad_state, share, sum1, sum2 = run_head(
        state, weights, sections * depth // HEAD_ROWS, b1, b2, labels[:, None], classes
    )
    grad_scaled = None
    parts = []
    for group in GROUPS:
        opening, closing = group is GROUPS[0], group is GROUPS[-1]
        made, grad_state, grad_scaled, *sums = run_backward(
            group, saved, weights, turned, masks, grad_state, grad_scaled,
            share if opening else None, features if closing else None, stats, total_rows,
        )
        parts.append(lax.psum_scatter(made, "fsdp", scatter_dimension=0))
    mine = [None] * sections
    for group, part in zip(GROUPS, parts):
        for at, n in enumerate(group):
            mine[n] = part[at * depth : (at + 1) * depth]
    mine = jnp.concatenate(mine + [parts[0][-HEAD_ROWS:]], 0)
    for flip in (1, 3):
        other = lax.ppermute(mine, names, pairs(sizes, 0, flip))
        mine = mine.astype(F32) + other.astype(F32)
        if flip == 1:
            mine = mine.astype(BF16)
    gate_grad = mine[: sections * depth].reshape(sections, depth, columns)
    head_grad = mine[sections * depth :]
    head_first_grad = head_grad[:, :hidden]
    head_second_grad = head_grad[: head_second.shape[0], hidden : hidden + classes]

    small = jnp.concatenate([sums[0].reshape(-1), sum1[0], sum2[0]])
    small = jnp.pad(small, (0, -small.size % 1024)).reshape(-1, LANES)
    small = everywhere_sum(small, sizes, names).reshape(-1)
    sum_grad, sum_cross = small[:width], small[width : 2 * width]
    first_bias_grad = small[2 * width : 2 * width + hidden]
    second_bias_grad = small[2 * width + hidden : 2 * width + hidden + classes]
    normed, scale = normalise(total_rows, features, stats)
    features_grad = (
        scale * gain * (grad_scaled - sum_grad / total_rows - normed * (sum_cross / total_rows))
    )
    return (
        features_grad,
        sum_cross,
        sum_grad,
        gate_grad,
        head_first_grad,
        first_bias_grad,
        head_second_grad,
        second_bias_grad,
    )


def solution(mesh):
    placed = (
        P(("dp", "fsdp"), None),
        P(),
        P(),
        P(None, "fsdp", None),
        P(),
        P("fsdp", None),
        P(),
        P("fsdp", None),
        P(),
        P(("dp", "fsdp")),
    )
    sizes = (mesh.shape["dp"], 4, 4, mesh.shape["fsdp"] // 16)
    return jax.shard_map(
        functools.partial(on_device, sizes),
        mesh=mesh,
        in_specs=placed,
        out_specs=(
            P(("dp", "fsdp"), None),
            P(),
            P(),
            P(None, "fsdp", None),
            P("fsdp", None),
            P(),
            P("fsdp", None),
            P(),
        ),
        check_vma=False,
    )
```

```python
import functools
import math

import jax
import jax.numpy as jnp
import numpy as np
from jax import lax
from jax.experimental import pallas as pl
from jax.experimental.pallas import tpu as pltpu
from jax.sharding import PartitionSpec as P

epsilon = 1e-05
F32 = jnp.float32
BF16 = jnp.bfloat16
VMEM_LIMIT = 60 * 1024 * 1024
HEAD_ROWS = 16
OPENING = 3
COLUMN = 2
LANES = 128


def sigmoid(value):
    return 0.5 * jnp.tanh(0.5 * value) + 0.5


def dot(left, right):
    return jnp.dot(left, right, preferred_element_type=F32)


def dot_cols(left, right):
    return lax.dot_general(left, right, (((1,), (1,)), ((), ())), preferred_element_type=F32)


def erf(value):
    value = jnp.clip(value, -4.0, 4.0)
    square = value * value
    top = jnp.full_like(square, -2.72614225801306e-10)
    for term in (
        2.77068142495902e-08,
        -2.10102402082508e-06,
        -5.69250639462346e-05,
        -7.34990630326855e-04,
        -2.95459980854025e-03,
        -1.60960333262415e-02,
    ):
        top = top * square + term
    low = jnp.full_like(square, -1.45660718464996e-05)
    for term in (
        -2.13374055278905e-04,
        -1.68282697438203e-03,
        -7.37332916720468e-03,
        -1.42647390514189e-02,
    ):
        low = low * square + term
    return value * top / low


def normalise(total_rows, features, stats):
    mean = stats[0:1] / total_rows
    scale = lax.rsqrt(stats[1:2] / total_rows - mean * mean + epsilon)
    return (features.astype(F32) - mean) * scale, scale


def halves(rows):
    return [slice(0, rows // 2), slice(rows // 2, rows)]


def section_weight(w_ref, slot, width):
    half = w_ref.shape[1] // 2

    def weight(lower, start):
        place = slice(0, half) if lower else slice(half, 2 * half)
        return w_ref[slot, place, :, :, start : start + width].reshape(width, width)

    return weight


def forward_section(mask, weight, slot, wide_ref, held_ref, state_ref, low_ref):
    rows, width = state_ref.shape
    mask = mask.astype(BF16)
    for part in halves(rows):
        state = state_ref[part]
        state_low = state.astype(BF16)
        masked = low_ref[part] * mask
        wide_ref[slot, part] = state
        reset = sigmoid(dot(state_low, weight(True, width)) + dot(masked, weight(False, width)))
        held_ref[slot, 1, part] = reset.astype(BF16)
        second = (reset * state).astype(BF16)
        update = sigmoid(dot(state_low, weight(True, 0)) + dot(masked, weight(False, 0)))
        held_ref[slot, 0, part] = update.astype(BF16)
        output = jnp.tanh(
            dot(second, weight(True, 2 * width)) + dot(masked, weight(False, 2 * width))
        )
        held_ref[slot, 2, part] = output.astype(BF16)
        state_ref[part] = state + update * (output - state)


def backward_rows(mask, weight, slot, wide_ref, held_ref, left_ref, grads_ref, grad_ref, scaled_ref):
    rows, width = grad_ref.shape
    for part in halves(rows):
        grad = grad_ref[part]
        state = wide_ref[slot, part]
        update, reset, output = [held_ref[slot, which, part].astype(F32) for which in range(3)]
        left_ref[0, :, part] = state.astype(BF16).T
        left_ref[1, :, part] = (reset * state).astype(BF16).T
        grad_output = (grad * update * (1.0 - output * output)).astype(BF16)
        grads_ref[part, 2 * width :] = grad_output
        grad_update = (grad * (output - state) * update * (1.0 - update)).astype(BF16)
        grads_ref[part, 0:width] = grad_update
        through = dot_cols(grad_output, weight(True, 2 * width))
        grad_reset = (through * state * reset * (1.0 - reset)).astype(BF16)
        grads_ref[part, width : 2 * width] = grad_reset
        grad_ref[part] = (
            grad * (1.0 - update)
            + through * reset
            + dot_cols(grad_update, weight(True, 0))
            + dot_cols(grad_reset, weight(True, width))
        )
        scaled_ref[part] += mask * (
            dot_cols(grad_update, weight(False, 0))
            + dot_cols(grad_reset, weight(False, width))
            + dot_cols(grad_output, weight(False, 2 * width))
        )


def backward_weights(mask, slot, left_ref, grads_ref, turned_ref, made_ref):
    width = turned_ref.shape[0]
    blocks, depth = made_ref.shape[1], made_ref.shape[3]
    column = jnp.broadcast_to(mask, (8, width)).T[:, 0:1]

    def put(place, columns, value):
        value = value.astype(BF16).reshape(blocks // 2, 2, depth, width)
        made_ref[slot, place, :, :, columns] = value

    for gate in range(3):
        columns = slice(gate * width, (gate + 1) * width)
        put(slice(0, blocks // 2), columns, dot(left_ref[gate // 2], grads_ref[:, columns]))
        put(
            slice(blocks // 2, blocks),
            columns,
            column * dot(turned_ref[...], grads_ref[:, columns]),
        )


def head_rows(
    row_scale, classes, state_ref, head_ref, b1_ref, b2_ref, label_ref,
    grad_ref, share_ref, sum1_ref, sum2_ref,
):
    rows, width = state_ref.shape
    blocks = head_ref.shape[0]
    owners = 2 * blocks
    hidden = b1_ref.shape[1]
    first = head_ref[:, :, :, 0:hidden].reshape(width, hidden)
    second = head_ref[:, :, :, hidden : hidden + LANES].astype(F32)[:, :, 0 : hidden // owners]
    second = second.reshape(hidden, LANES).astype(BF16)
    head_in = state_ref[...].astype(BF16)
    pre = dot(head_in, first) + b1_ref[...]
    phi = 0.5 + 0.5 * erf(pre * math.sqrt(0.5))
    activation = (pre * phi).astype(BF16)
    slope = phi + pre * (jnp.exp(-0.5 * pre * pre) * (1.0 / math.sqrt(2.0 * math.pi)))
    lane = lax.broadcasted_iota(jnp.int32, (rows, LANES), 1)
    logits = dot(activation, second) + b2_ref[...]
    logits = jnp.where(lane < classes, logits, -1e30)
    powers = jnp.exp(logits - jnp.max(logits, 1, keepdims=True))
    chance = powers / jnp.sum(powers, 1, keepdims=True)
    hit = jnp.where(lane == label_ref[...], 1.0, 0.0)
    grad_logits = ((chance - hit) * row_scale).astype(BF16)
    sum2_ref[...] = jnp.sum(grad_logits.astype(F32), 0, keepdims=True)
    grad_second = dot(activation.T, grad_logits)
    grad_pre = (dot_cols(grad_logits, second) * slope).astype(BF16)
    sum1_ref[...] = jnp.sum(grad_pre.astype(F32), 0, keepdims=True)
    grad_first = dot(head_in.T, grad_pre)
    grad_ref[...] = dot_cols(grad_pre, first)
    grad_second = grad_second.reshape(blocks, 2, hidden // owners, LANES)
    grad_second = jnp.concatenate([grad_second, jnp.zeros_like(grad_second)], 2)
    share_ref[:, :, :, 0:hidden] = grad_first.reshape(blocks, 2, HEAD_ROWS, hidden).astype(BF16)
    share_ref[:, :, :, hidden : hidden + LANES] = grad_second.astype(BF16)
    tail = share_ref.shape[3] - hidden - LANES
    share_ref[:, :, :, hidden + LANES :] = jnp.zeros((blocks, 2, HEAD_ROWS, tail), BF16)


def upper_kernel(
    total_rows, classes,
    x_ref, stat_ref, gain_ref, bias_ref, mask_ref, b1_ref, b2_ref, label_ref, weights,
    s_out, u_out, r_out, o_out, turned_out, grad_out, scaled_out, made_out, sum1_ref, sum2_ref,
    wide_ref, held_ref, w_ref, head_ref, low_ref, turned_ref, state_ref, scaled_ref,
    share_ref, made_ref, left_ref, grads_ref, w_sem, save_sem, made_sem, out_sem,
):
    rows, width = x_ref.shape
    sections = mask_ref.shape[0]
    depth = w_ref.shape[3]
    stored = sections - OPENING

    def slot_of(n):
        return jnp.where(n < stored, lax.rem(n, 2), n - stored + 2)

    def w_copy(n):
        rows_at = pl.ds(pl.multiple_of(n * depth, depth), depth)
        slot = slot_of(n)
        return pltpu.make_async_copy(weights.at[:, :, rows_at, :], w_ref.at[slot], w_sem.at[slot])

    head_copy = pltpu.make_async_copy(
        weights.at[:, :, pl.ds(sections * depth, HEAD_ROWS), pl.ds(0, head_ref.shape[3])],
        head_ref,
        out_sem.at[0],
    )

    def save_copies(n, slot):
        return [pltpu.make_async_copy(wide_ref.at[slot], s_out.at[n], save_sem.at[slot, 0])] + [
            pltpu.make_async_copy(held_ref.at[slot, at], out.at[n], save_sem.at[slot, at + 1])
            for at, out in enumerate((u_out, r_out, o_out))
        ]

    def made_copy(at):
        rows_at = pl.ds(pl.multiple_of(at * depth, depth), depth)
        slot = lax.rem(at, 2)
        return pltpu.make_async_copy(
            made_ref.at[slot], made_out.at[:, :, rows_at, :], made_sem.at[slot]
        )

    share_copy = pltpu.make_async_copy(
        share_ref, made_out.at[:, :, pl.ds(OPENING * depth, HEAD_ROWS), :], out_sem.at[1]
    )
    turned_copy = pltpu.make_async_copy(turned_ref, turned_out, out_sem.at[2])
    last_copies = [
        pltpu.make_async_copy(state_ref, grad_out, out_sem.at[3]),
        pltpu.make_async_copy(scaled_ref, scaled_out, out_sem.at[4]),
    ]

    w_copy(0).start()
    w_copy(1).start()
    head_copy.start()
    for part in halves(rows):
        normed, _ = normalise(total_rows, x_ref[part], stat_ref[...])
        scaled = normed * gain_ref[...] + bias_ref[...]
        state_ref[part] = scaled
        low = scaled.astype(BF16)
        low_ref[part] = low
        turned_ref[:, part] = low.T
    turned_copy.start()

    def forward(n, carry):
        slot = slot_of(n)
        w_copy(n).wait()

        @pl.when((n >= 1) & (n + 1 < sections))
        def _():
            w_copy(n + 1).start()

        @pl.when((n >= 2) & (n < stored))
        def _():
            for copy in save_copies(n - 2, slot):
                copy.wait()

        forward_section(
            mask_ref[n], section_weight(w_ref, slot, width), slot,
            wide_ref, held_ref, state_ref, low_ref,
        )

        @pl.when(n < stored)
        def _():
            for copy in save_copies(n, slot):
                copy.start()

        return carry

    lax.fori_loop(0, sections, forward, 0)
    head_copy.wait()
    head_rows(
        1.0 / rows, classes, state_ref, head_ref, b1_ref, b2_ref, label_ref,
        state_ref, share_ref, sum1_ref, sum2_ref,
    )
    share_copy.start()
    scaled_ref[...] = jnp.zeros_like(scaled_ref)

    def backward(at, carry):
        n = sections - 1 - at
        slot = slot_of(n)
        backward_rows(
            mask_ref[n], section_weight(w_ref, slot, width), slot,
            wide_ref, held_ref, left_ref, grads_ref, state_ref, scaled_ref,
        )

        @pl.when(at == OPENING - 1)
        def _():
            for copy in last_copies:
                copy.start()

        @pl.when(at >= 2)
        def _():
            made_copy(at - 2).wait()

        backward_weights(
            mask_ref[n], lax.rem(at, 2), left_ref, grads_ref, turned_ref, made_ref
        )
        made_copy(at).start()
        return carry

    lax.fori_loop(0, OPENING, backward, 0)
    for n in range(max(stored - 2, 0), stored):
        for copy in save_copies(n, n % 2):
            copy.wait()
    for at in (OPENING - 2, OPENING - 1):
        made_copy(at).wait()
    for copy in [share_copy, turned_copy, *last_copies]:
        copy.wait()


def run_upper(features, stats, gain, bias, masks, b1, b2, labels, weights, classes, total_rows):
    rows, width = features.shape
    sections = masks.shape[0]
    blocks = weights.shape[0]
    depth = width // blocks
    hidden = b1.shape[1]
    stored = sections - OPENING
    slots = 2 + OPENING
    anywhere = pl.BlockSpec(memory_space=pl.ANY)
    inside = pl.BlockSpec(memory_space=pltpu.VMEM)
    tall = jax.ShapeDtypeStruct((rows, width), F32)
    saved = [jax.ShapeDtypeStruct((stored, rows, width), kind) for kind in (F32, BF16, BF16, BF16)]
    return pl.pallas_call(
        functools.partial(upper_kernel, total_rows, classes),
        in_specs=[inside] * 8 + [anywhere],
        out_specs=[anywhere] * 8 + [inside] * 2,
        out_shape=saved
        + [
            jax.ShapeDtypeStruct((width, rows), BF16),
            tall,
            tall,
            jax.ShapeDtypeStruct((blocks, 2, OPENING * depth + HEAD_ROWS, 3 * width), BF16),
            jax.ShapeDtypeStruct((1, hidden), F32),
            jax.ShapeDtypeStruct((1, LANES), F32),
        ],
        scratch_shapes=[
            pltpu.VMEM((slots, rows, width), F32),
            pltpu.VMEM((slots, 3, rows, width), BF16),
            pltpu.VMEM((slots, blocks, 2, depth, 3 * width), BF16),
            pltpu.VMEM((blocks, 2, HEAD_ROWS, hidden + LANES), BF16),
            pltpu.VMEM((rows, width), BF16),
            pltpu.VMEM((width, rows), BF16),
            pltpu.VMEM((rows, width), F32),
            pltpu.VMEM((rows, width), F32),
            pltpu.VMEM((blocks, 2, HEAD_ROWS, 3 * width), BF16),
            pltpu.VMEM((2, blocks, 2, depth, 3 * width), BF16),
            pltpu.VMEM((2, width, rows), BF16),
            pltpu.VMEM((rows, 3 * width), BF16),
            pltpu.SemaphoreType.DMA((slots,)),
            pltpu.SemaphoreType.DMA((2, 4)),
            pltpu.SemaphoreType.DMA((2,)),
            pltpu.SemaphoreType.DMA((5,)),
        ],
        compiler_params=pltpu.CompilerParams(vmem_limit_bytes=VMEM_LIMIT),
        name="sections_and_head",
    )(features, stats, gain, bias, masks, b1, b2, labels, weights)


def lower_kernel(
    total_rows,
    place_ref, mask_ref, x_ref, stat_ref, s_in, u_in, r_in, o_in, weights, turned_in, grad_in, scaled_in,
    own_x, pass_x, own_zy, pass_zy, total_out, sums_ref,
    wide_ref, held_ref, w_ref, turned_ref, grad_ref, scaled_ref,
    made_ref, left_ref, grads_ref, load_sem, in_sem, made_sem, out_sem,
):
    rows, width = grad_ref.shape
    depth = w_ref.shape[3]
    count = s_in.shape[0]
    core = place_ref[2]
    quarter = own_x.shape[3]

    def load_copies(at):
        n, slot = count - 1 - at, lax.rem(at, 2)
        rows_at = pl.ds(pl.multiple_of(n * depth, depth), depth)
        return [
            pltpu.make_async_copy(s_in.at[n], wide_ref.at[slot], load_sem.at[slot, 0]),
            *[
                pltpu.make_async_copy(array.at[n], held_ref.at[slot, which], load_sem.at[slot, 1 + which])
                for which, array in enumerate((u_in, r_in, o_in))
            ],
            pltpu.make_async_copy(weights.at[:, :, rows_at, :], w_ref.at[slot], load_sem.at[slot, 4]),
        ]

    def column_copies(at, slot):
        rows_at = pl.ds(pl.multiple_of(at * depth, depth), depth)
        return [
            pltpu.make_async_copy(
                made_ref.at[slot, :, side, :, pl.ds(q * quarter, quarter)],
                out.at[q, :, rows_at, :],
                made_sem.at[slot, which, q],
            )
            for which, (side, out) in enumerate(((core, own_x), (1 - core, pass_x)))
            for q in range(4)
        ]

    def plane_copies(at, slot):
        rows_at = pl.ds(pl.multiple_of(at * depth, depth), depth)
        return [
            pltpu.make_async_copy(
                made_ref.at[slot, :, side], out.at[:, rows_at, :], made_sem.at[slot, which, 0]
            )
            for which, (side, out) in enumerate(((core, own_zy), (1 - core, pass_zy)))
        ]

    grad_copy = pltpu.make_async_copy(grad_in, grad_ref, in_sem.at[0])
    scaled_copy = pltpu.make_async_copy(scaled_in, scaled_ref, in_sem.at[1])
    turned_copy = pltpu.make_async_copy(turned_in, turned_ref, in_sem.at[2])
    total_copy = pltpu.make_async_copy(scaled_ref, total_out, out_sem.at[0])
    grad_copy.start()
    for copy in load_copies(0):
        copy.start()
    scaled_copy.start()
    turned_copy.start()
    grad_copy.wait()

    def backward(at, carry):
        n, slot = count - 1 - at, lax.rem(at, 2)
        for copy in load_copies(at):
            copy.wait()

        @pl.when(at == 0)
        def _():
            scaled_copy.wait()

        @pl.when(at + 1 < count)
        def _():
            for copy in load_copies(at + 1):
                copy.start()

        backward_rows(
            mask_ref[n], section_weight(w_ref, slot, width), slot,
            wide_ref, held_ref, left_ref, grads_ref, grad_ref, scaled_ref,
        )

        @pl.when(at == 0)
        def _():
            turned_copy.wait()

        @pl.when((at >= 2) & (at - 2 < COLUMN))
        def _():
            for copy in column_copies(at - 2, slot):
                copy.wait()

        @pl.when(at - 2 >= COLUMN)
        def _():
            for copy in plane_copies(at - 2 - COLUMN, slot):
                copy.wait()

        @pl.when(at == count - 1)
        def _():
            total = scaled_ref[...] + grad_ref[...]
            scaled_ref[...] = total
            normed, _ = normalise(total_rows, x_ref[...], stat_ref[...])
            sums_ref[0:1] = jnp.sum(total, 0, keepdims=True)
            sums_ref[1:2] = jnp.sum(total * normed, 0, keepdims=True)
            total_copy.start()

        backward_weights(mask_ref[n], slot, left_ref, grads_ref, turned_ref, made_ref)

        @pl.when(at < COLUMN)
        def _():
            for copy in column_copies(at, slot):
                copy.start()

        @pl.when(at >= COLUMN)
        def _():
            for copy in plane_copies(at - COLUMN, slot):
                copy.start()

        return carry

    lax.fori_loop(0, count, backward, 0)
    for at in range(max(count - 2, 0), count):
        copies = column_copies(at, at % 2) if at < COLUMN else plane_copies(at - COLUMN, at % 2)
        for copy in copies:
            copy.wait()
    total_copy.wait()


def run_lower(place, masks, features, stats, saved, weights, turned, grad_state, grad_scaled, total_rows):
    rows, width = features.shape
    blocks = weights.shape[0]
    depth = width // blocks
    count = saved[0].shape[0]
    columns = 3 * width
    anywhere = pl.BlockSpec(memory_space=pl.ANY)
    inside = pl.BlockSpec(memory_space=pltpu.VMEM)
    across = jax.ShapeDtypeStruct((4, blocks, COLUMN * depth, columns // 4), BF16)
    plane = jax.ShapeDtypeStruct((blocks, (count - COLUMN) * depth, columns), BF16)
    return pl.pallas_call(
        functools.partial(lower_kernel, total_rows),
        in_specs=[pl.BlockSpec(memory_space=pltpu.SMEM)] + [inside] * 3 + [anywhere] * 8,
        out_specs=[anywhere] * 5 + [inside],
        out_shape=[
            across,
            across,
            plane,
            plane,
            jax.ShapeDtypeStruct((rows, width), F32),
            jax.ShapeDtypeStruct((2, width), F32),
        ],
        scratch_shapes=[
            pltpu.VMEM((2, rows, width), F32),
            pltpu.VMEM((2, 3, rows, width), BF16),
            pltpu.VMEM((2, blocks, 2, depth, columns), BF16),
            pltpu.VMEM((width, rows), BF16),
            pltpu.VMEM((rows, width), F32),
            pltpu.VMEM((rows, width), F32),
            pltpu.VMEM((2, blocks, 2, depth, columns), BF16),
            pltpu.VMEM((2, width, rows), BF16),
            pltpu.VMEM((rows, columns), BF16),
            pltpu.SemaphoreType.DMA((2, 5)),
            pltpu.SemaphoreType.DMA((3,)),
            pltpu.SemaphoreType.DMA((2, 2, 4)),
            pltpu.SemaphoreType.DMA((1,)),
        ],
        compiler_params=pltpu.CompilerParams(vmem_limit_bytes=VMEM_LIMIT),
        name="sections_backward",
    )(place, masks, features, stats, *saved, weights, turned, grad_state, grad_scaled)


def pairs(sizes, axis, flip):
    table = []
    for source in range(math.prod(sizes)):
        place = list(np.unravel_index(source, sizes))
        place[axis] ^= flip
        table.append((source, int(np.ravel_multi_index(place, sizes))))
    return table


def everywhere_sum(value, sizes, names):
    for axis in reversed(range(len(sizes))):
        for flip in (1, 3) if sizes[axis] == 4 else (1,):
            value = value + lax.ppermute(value, names, pairs(sizes, axis, flip))
    return value


def add(*parts):
    return functools.reduce(lambda a, b: a + b, [part.astype(F32) for part in parts])


def shifted(sizes, axis, by):
    table = []
    for source in range(math.prod(sizes)):
        place = list(np.unravel_index(source, sizes))
        place[axis] = (place[axis] + by) % sizes[axis]
        table.append((source, int(np.ravel_multi_index(place, sizes))))
    return table


def in_order(parts, at):
    turned = jnp.stack(parts[::-1] * 2, 0)
    return lax.dynamic_slice_in_dim(turned, 3 - at, 4, 0)


def column_scatter(total):
    got = lax.all_to_all(total, "dp", 0, 0)
    return jnp.sum(got.astype(F32), 0).astype(BF16)


def plane_scatter(total):
    groups = [[2 * at + core for at in range(total.shape[0])] for core in range(2)]
    got = lax.all_to_all(total, "fsdp", 0, 0, axis_index_groups=groups)
    return jnp.sum(got.astype(F32), 0).astype(BF16)


def column_gather(part, sizes, names, place):
    parts = [part] + [lax.ppermute(part, names, shifted(sizes, 0, by)) for by in (1, 2, 3)]
    return jnp.concatenate(list(in_order(parts, place[3])), 1).astype(F32)


def permute_scatter(total, sizes, names, place):
    total = total.reshape(sizes[1], sizes[2], *total.shape[1:])
    for axis in (1, 2):
        pick = lambda by: lax.dynamic_index_in_dim(
            total, (place[axis - 1] + by) % sizes[axis], 0, keepdims=False
        )
        arrived = [lax.ppermute(pick(by), names, shifted(sizes, axis, by)) for by in (1, 3, 2)]
        total = add(pick(0), *arrived).astype(BF16)
    return total


def column_sum(value, sizes, names):
    for flip in (1, 3):
        other = lax.ppermute(value, names, pairs(sizes, 0, flip))
        value = add(value, other)
        if flip == 1:
            value = value.astype(BF16)
    return value


def on_device(
    sizes,
    features,
    bn_gain,
    bn_bias,
    gate_weights,
    feature_masks,
    head_first,
    head_first_bias,
    head_second,
    head_second_bias,
    labels,
):
    names = ("dp", "fsdp")
    rows, width = features.shape
    sections, depth, columns = gate_weights.shape
    hidden = head_first.shape[1]
    classes = head_second.shape[1]
    total_rows = rows * math.prod(sizes)
    gain, bias = bn_gain[None], bn_bias[None]
    masks = feature_masks.astype(F32)[:, None, :]
    b1 = head_first_bias[None]
    b2 = jnp.pad(head_second_bias, (0, LANES - classes))[None]

    inputs = features.astype(F32)
    stats = jnp.stack([jnp.sum(inputs, 0), jnp.sum(inputs * inputs, 0)])
    stats = everywhere_sum(stats.reshape(-1, LANES), sizes, names).reshape(2, width)

    extra = jnp.pad(head_first, ((0, 0), (0, columns - hidden))) + jnp.pad(
        head_second, ((0, HEAD_ROWS - head_second.shape[0]), (hidden, columns - hidden - classes))
    )
    weights = lax.all_gather(
        jnp.concatenate([gate_weights.reshape(sections * depth, columns), extra], 0), "fsdp", axis=0
    )
    weights = weights.reshape(-1, 2, *weights.shape[1:])
    fsdp = lax.axis_index("fsdp")
    place = jnp.stack([fsdp // 8, fsdp // 2 % 4, fsdp % 2, lax.axis_index("dp")])
    *saved, turned, grad_state, grad_scaled, top, sum1, sum2 = run_upper(
        features, stats, gain, bias, masks, b1, b2, labels[:, None], weights, classes, total_rows
    )
    top = lax.psum_scatter(top.reshape(-1, *top.shape[2:]), "fsdp", scatter_dimension=0)
    own_x, pass_x, own_zy, pass_zy, grad_scaled, *sums = run_lower(
        place, masks, features, stats, saved, weights, turned, grad_state, grad_scaled, total_rows
    )
    across = add(own_x, lax.ppermute(pass_x, names, pairs(sizes, 3, 1))).astype(BF16)
    plane = add(own_zy, lax.ppermute(pass_zy, names, pairs(sizes, 3, 1))).astype(BF16)
    across, plane, sums = lax.optimization_barrier((across, plane, sums))
    across = column_scatter(across)
    plane = permute_scatter(plane, sizes, names, place)
    small = jnp.concatenate([sums[0].reshape(-1), sum1[0], sum2[0]])
    small = jnp.pad(small, (0, -small.size % 1024)).reshape(-1, LANES)
    small = everywhere_sum(small, sizes, names).reshape(-1)
    across = column_gather(plane_scatter(across), sizes, names, place)
    plane = column_sum(plane, sizes, names)
    small, top = lax.optimization_barrier((small, top))
    top = column_sum(top, sizes, names)
    finished = [None] * sections
    order = list(range(sections))[::-1]
    cuts = (OPENING, OPENING + COLUMN, sections)
    for part, start, stop in zip((top, across, plane), (0, *cuts), cuts):
        for at, n in enumerate(order[start:stop]):
            finished[n] = part[at * depth : (at + 1) * depth]
    head_grad = top[OPENING * depth :]
    gate_grad = jnp.stack(finished, 0)
    head_first_grad = head_grad[:, :hidden]
    head_second_grad = head_grad[: head_second.shape[0], hidden : hidden + classes]

    sum_grad, sum_cross = small[:width], small[width : 2 * width]
    first_bias_grad = small[2 * width : 2 * width + hidden]
    second_bias_grad = small[2 * width + hidden : 2 * width + hidden + classes]
    normed, scale = normalise(total_rows, features, stats)
    features_grad = (
        scale * gain * (grad_scaled - sum_grad / total_rows - normed * (sum_cross / total_rows))
    )
    return (
        features_grad,
        sum_cross,
        sum_grad,
        gate_grad,
        head_first_grad,
        first_bias_grad,
        head_second_grad,
        second_bias_grad,
    )


def solution(mesh):
    placed = (
        P(("dp", "fsdp"), None),
        P(),
        P(),
        P(None, "fsdp", None),
        P(),
        P("fsdp", None),
        P(),
        P("fsdp", None),
        P(),
        P(("dp", "fsdp")),
    )
    sizes = (mesh.shape["dp"], 4, 4, mesh.shape["fsdp"] // 16)
    return jax.shard_map(
        functools.partial(on_device, sizes),
        mesh=mesh,
        in_specs=placed,
        out_specs=(
            P(("dp", "fsdp"), None),
            P(),
            P(),
            P(None, "fsdp", None),
            P("fsdp", None),
            P(),
            P("fsdp", None),
            P(),
        ),
        check_vma=False,
    )
```

```python
import functools
import math

import jax
import jax.numpy as jnp
import numpy as np
from jax import lax
from jax.experimental import pallas as pl
from jax.experimental.pallas import tpu as pltpu
from jax.sharding import PartitionSpec as P

epsilon = 1e-05
F32 = jnp.float32
BF16 = jnp.bfloat16
VMEM_LIMIT = 60 * 1024 * 1024
HEAD_ROWS = 16
OPENING = 4
QUARTERS = ((0, 0, 4), (1, 0, 4), (3, 0, 4), (2, 0, 2), (2, 2, 4))
PIECES = 2 * len(QUARTERS)
LANES = 128


def sigmoid(value):
    return 0.5 * jnp.tanh(0.5 * value) + 0.5


def dot(left, right):
    return jnp.dot(left, right, preferred_element_type=F32)


def dot_cols(left, right):
    return lax.dot_general(left, right, (((1,), (1,)), ((), ())), preferred_element_type=F32)


def erf(value):
    value = jnp.clip(value, -4.0, 4.0)
    square = value * value
    top = jnp.full_like(square, -2.72614225801306e-10)
    for term in (
        2.77068142495902e-08,
        -2.10102402082508e-06,
        -5.69250639462346e-05,
        -7.34990630326855e-04,
        -2.95459980854025e-03,
        -1.60960333262415e-02,
    ):
        top = top * square + term
    low = jnp.full_like(square, -1.45660718464996e-05)
    for term in (
        -2.13374055278905e-04,
        -1.68282697438203e-03,
        -7.37332916720468e-03,
        -1.42647390514189e-02,
    ):
        low = low * square + term
    return value * top / low


def normalise(total_rows, features, stats):
    mean = stats[0:1] / total_rows
    scale = lax.rsqrt(stats[1:2] / total_rows - mean * mean + epsilon)
    return (features.astype(F32) - mean) * scale, scale


def halves(rows):
    return [slice(0, rows // 2), slice(rows // 2, rows)]


def section_weight(w_ref, slot, width):
    half = w_ref.shape[1] // 2

    def weight(lower, start):
        place = slice(0, half) if lower else slice(half, 2 * half)
        return w_ref[slot, place, ..., start : start + width].reshape(width, width)

    return weight


def forward_section(mask, weight, slot, wide_ref, held_ref, state_ref, low_ref):
    rows, width = state_ref.shape
    mask = mask.astype(BF16)
    for part in halves(rows):
        state = state_ref[part]
        state_low = state.astype(BF16)
        masked = low_ref[part] * mask
        wide_ref[slot, part] = state
        reset = sigmoid(dot(state_low, weight(True, width)) + dot(masked, weight(False, width)))
        held_ref[slot, 1, part] = reset.astype(BF16)
        second = (reset * state).astype(BF16)
        update = sigmoid(dot(state_low, weight(True, 0)) + dot(masked, weight(False, 0)))
        held_ref[slot, 0, part] = update.astype(BF16)
        output = jnp.tanh(
            dot(second, weight(True, 2 * width)) + dot(masked, weight(False, 2 * width))
        )
        held_ref[slot, 2, part] = output.astype(BF16)
        state_ref[part] = state + update * (output - state)


def backward_rows(mask, weight, slot, wide_ref, held_ref, left_ref, grads_ref, grad_ref, scaled_ref):
    rows, width = grad_ref.shape
    for part in halves(rows):
        grad = grad_ref[part]
        state = wide_ref[slot, part]
        update, reset, output = [held_ref[slot, which, part].astype(F32) for which in range(3)]
        left_ref[0, :, part] = state.astype(BF16).T
        left_ref[1, :, part] = (reset * state).astype(BF16).T
        grad_output = (grad * update * (1.0 - output * output)).astype(BF16)
        grads_ref[part, 2 * width :] = grad_output
        grad_update = (grad * (output - state) * update * (1.0 - update)).astype(BF16)
        grads_ref[part, 0:width] = grad_update
        through = dot_cols(grad_output, weight(True, 2 * width))
        grad_reset = (through * state * reset * (1.0 - reset)).astype(BF16)
        grads_ref[part, width : 2 * width] = grad_reset
        grad_ref[part] = (
            grad * (1.0 - update)
            + through * reset
            + dot_cols(grad_update, weight(True, 0))
            + dot_cols(grad_reset, weight(True, width))
        )
        scaled_ref[part] += mask * (
            dot_cols(grad_update, weight(False, 0))
            + dot_cols(grad_reset, weight(False, width))
            + dot_cols(grad_output, weight(False, 2 * width))
        )


def backward_weights(mask, slot, left_ref, grads_ref, turned_ref, made_ref):
    width = turned_ref.shape[0]
    blocks, depth = made_ref.shape[1], made_ref.shape[3]
    column = jnp.broadcast_to(mask, (8, width)).T[:, 0:1]

    def put(place, columns, value):
        value = value.astype(BF16).reshape(blocks // 2, 2, depth, width)
        made_ref[slot, place, :, :, columns] = value

    for gate in range(3):
        columns = slice(gate * width, (gate + 1) * width)
        put(slice(0, blocks // 2), columns, dot(left_ref[gate // 2], grads_ref[:, columns]))
        put(
            slice(blocks // 2, blocks),
            columns,
            column * dot(turned_ref[...], grads_ref[:, columns]),
        )


def head_rows(
    row_scale, classes, state_ref, head_ref, b1_ref, b2_ref, label_ref,
    grad_ref, share_ref, sum1_ref, sum2_ref,
):
    rows, width = state_ref.shape
    blocks = share_ref.shape[0]
    owners = 2 * blocks
    hidden = b1_ref.shape[1]
    first = head_ref[..., 0:hidden].reshape(width, hidden)
    second = head_ref[..., hidden : hidden + LANES].astype(F32)[..., 0 : hidden // owners, :]
    second = second.reshape(hidden, LANES).astype(BF16)
    head_in = state_ref[...].astype(BF16)
    pre = dot(head_in, first) + b1_ref[...]
    phi = 0.5 + 0.5 * erf(pre * math.sqrt(0.5))
    activation = (pre * phi).astype(BF16)
    slope = phi + pre * (jnp.exp(-0.5 * pre * pre) * (1.0 / math.sqrt(2.0 * math.pi)))
    lane = lax.broadcasted_iota(jnp.int32, (rows, LANES), 1)
    logits = dot(activation, second) + b2_ref[...]
    logits = jnp.where(lane < classes, logits, -1e30)
    powers = jnp.exp(logits - jnp.max(logits, 1, keepdims=True))
    chance = powers / jnp.sum(powers, 1, keepdims=True)
    hit = jnp.where(lane == label_ref[...], 1.0, 0.0)
    grad_logits = ((chance - hit) * row_scale).astype(BF16)
    sum2_ref[...] = jnp.sum(grad_logits.astype(F32), 0, keepdims=True)
    grad_second = dot(activation.T, grad_logits)
    grad_pre = (dot_cols(grad_logits, second) * slope).astype(BF16)
    sum1_ref[...] = jnp.sum(grad_pre.astype(F32), 0, keepdims=True)
    grad_first = dot(head_in.T, grad_pre)
    grad_ref[...] = dot_cols(grad_pre, first)
    grad_second = grad_second.reshape(blocks, 2, hidden // owners, LANES)
    grad_second = jnp.concatenate([grad_second, jnp.zeros_like(grad_second)], 2)
    share_ref[:, :, :, 0:hidden] = grad_first.reshape(blocks, 2, HEAD_ROWS, hidden).astype(BF16)
    share_ref[:, :, :, hidden : hidden + LANES] = grad_second.astype(BF16)
    tail = share_ref.shape[3] - hidden - LANES
    share_ref[:, :, :, hidden + LANES :] = jnp.zeros((blocks, 2, HEAD_ROWS, tail), BF16)


def entry_kernel(
    total_rows, place_ref, x_ref, stat_ref, gain_ref, bias_ref, mask_ref, *refs,
):
    pieces, refs = refs[:PIECES], refs[PIECES:]
    s_out, u_out, r_out, o_out, state_out, low_out, turned_out, full_out = refs[:8]
    wide_ref, held_ref, w_ref, low_ref, turned_ref, state_ref, w_sem, save_sem, out_sem = refs[8:]
    rows, width = x_ref.shape
    count, depth = w_ref.shape[0], w_ref.shape[4]
    quarter = w_ref.shape[5] // 4

    def piece_copies(at):
        copies = []
        for which, piece in enumerate(pieces):
            (by, first, last), side = QUARTERS[which // 2], which % 2
            core = place_ref[2] if side == 0 else 1 - place_ref[2]
            start = pl.multiple_of(lax.rem(place_ref[3] + 4 - by, 4) * quarter, LANES)
            copies.append(
                pltpu.make_async_copy(
                    piece.at[:, :, pl.ds(at * depth, depth)],
                    w_ref.at[at, first:last, :, core, :, pl.ds(start, quarter)],
                    w_sem.at[at, which],
                )
            )
        return copies

    def save_copies(at):
        return [
            pltpu.make_async_copy(w_ref.at[at], full_out.at[:, :, :, at], save_sem.at[at, 0]),
            pltpu.make_async_copy(wide_ref.at[at], s_out.at[at], save_sem.at[at, 1]),
        ] + [
            pltpu.make_async_copy(held_ref.at[at, which], out.at[at], save_sem.at[at, which + 2])
            for which, out in enumerate((u_out, r_out, o_out))
        ]

    out_copies = [
        pltpu.make_async_copy(low_ref, low_out, out_sem.at[0]),
        pltpu.make_async_copy(turned_ref, turned_out, out_sem.at[1]),
        pltpu.make_async_copy(state_ref, state_out, out_sem.at[2]),
    ]
    for at in range(count):
        for copy in piece_copies(at):
            copy.start()
    for part in halves(rows):
        normed, _ = normalise(total_rows, x_ref[part], stat_ref[...])
        scaled = normed * gain_ref[...] + bias_ref[...]
        state_ref[part] = scaled
        low = scaled.astype(BF16)
        low_ref[part] = low
        turned_ref[:, part] = low.T
    for copy in out_copies[:2]:
        copy.start()
    for at in range(count):
        for copy in piece_copies(at):
            copy.wait()
        forward_section(
            mask_ref[at], section_weight(w_ref, at, width), at,
            wide_ref, held_ref, state_ref, low_ref,
        )
        for copy in save_copies(at):
            copy.start()
    out_copies[2].start()
    for at in range(count):
        for copy in save_copies(at):
            copy.wait()
    for copy in out_copies:
        copy.wait()


def run_entry(place, features, stats, gain, bias, masks, pieces, count, total_rows):
    rows, width = features.shape
    depth = pieces[2].shape[2] // count
    anywhere = pl.BlockSpec(memory_space=pl.ANY)
    inside = pl.BlockSpec(memory_space=pltpu.VMEM)
    return pl.pallas_call(
        functools.partial(entry_kernel, total_rows),
        in_specs=[pl.BlockSpec(memory_space=pltpu.SMEM)] + [inside] * 5 + [anywhere] * PIECES,
        out_specs=[anywhere] * 8,
        out_shape=[
            jax.ShapeDtypeStruct((count, rows, width), kind) for kind in (F32, BF16, BF16, BF16)
        ]
        + [
            jax.ShapeDtypeStruct((rows, width), F32),
            jax.ShapeDtypeStruct((rows, width), BF16),
            jax.ShapeDtypeStruct((width, rows), BF16),
            jax.ShapeDtypeStruct((4, 4, 2, count, depth, 3 * width), BF16),
        ],
        scratch_shapes=[
            pltpu.VMEM((count, rows, width), F32),
            pltpu.VMEM((count, 3, rows, width), BF16),
            pltpu.VMEM((count, 4, 4, 2, depth, 3 * width), BF16),
            pltpu.VMEM((rows, width), BF16),
            pltpu.VMEM((width, rows), BF16),
            pltpu.VMEM((rows, width), F32),
            pltpu.SemaphoreType.DMA((count, PIECES)),
            pltpu.SemaphoreType.DMA((count, 5)),
            pltpu.SemaphoreType.DMA((3,)),
        ],
        compiler_params=pltpu.CompilerParams(vmem_limit_bytes=VMEM_LIMIT),
        name="first_sections",
    )(place, features, stats, gain, bias, masks, *pieces)


def upper_kernel(
    row_scale, classes,
    place_ref, mask_ref, b1_ref, b2_ref, label_ref, weights, state_in, low_in, turned_in, head_own, head_other,
    grad_out, scaled_out, made_out, sum1_ref, sum2_ref,
    wide_ref, held_ref, w_ref, head_ref, low_ref, turned_ref, state_ref, scaled_ref,
    share_ref, made_ref, left_ref, grads_ref, w_sem, made_sem, in_sem, out_sem,
):
    rows, width = state_ref.shape
    depth = w_ref.shape[3]
    early = mask_ref.shape[0] - OPENING

    def w_copy(n):
        rows_at = pl.ds(pl.multiple_of(n * depth, depth), depth)
        return pltpu.make_async_copy(weights.at[:, :, rows_at, :], w_ref.at[n], w_sem.at[n])

    def made_copy(at):
        rows_at = pl.ds(pl.multiple_of(at * depth, depth), depth)
        slot = lax.rem(at, 2)
        return pltpu.make_async_copy(
            made_ref.at[slot], made_out.at[:, :, rows_at, :], made_sem.at[slot]
        )

    head_rows_at = pl.ds(head_own.shape[2] - HEAD_ROWS, HEAD_ROWS)
    in_copies = [
        pltpu.make_async_copy(state_in, state_ref, in_sem.at[0]),
        pltpu.make_async_copy(low_in, low_ref, in_sem.at[1]),
        pltpu.make_async_copy(turned_in, turned_ref, in_sem.at[2]),
    ] + [
        pltpu.make_async_copy(
            array.at[:, :, head_rows_at], head_ref.at[:, :, side], in_sem.at[3 + which]
        )
        for which, (array, side) in enumerate(
            ((head_own, place_ref[2]), (head_other, 1 - place_ref[2]))
        )
    ]
    share_copy = pltpu.make_async_copy(
        share_ref, made_out.at[:, :, pl.ds(OPENING * depth, HEAD_ROWS), :], out_sem.at[0]
    )
    last_copies = [
        pltpu.make_async_copy(state_ref, grad_out, out_sem.at[1]),
        pltpu.make_async_copy(scaled_ref, scaled_out, out_sem.at[2]),
    ]
    for copy in in_copies[:2]:
        copy.start()
    w_copy(0).start()
    w_copy(1).start()
    for copy in in_copies[2:]:
        copy.start()
    for copy in in_copies[:2]:
        copy.wait()

    def forward(n, carry):
        w_copy(n).wait()

        @pl.when((n >= 1) & (n + 1 < OPENING))
        def _():
            w_copy(n + 1).start()

        forward_section(
            mask_ref[early + n], section_weight(w_ref, n, width), n,
            wide_ref, held_ref, state_ref, low_ref,
        )
        return carry

    lax.fori_loop(0, OPENING, forward, 0)
    for copy in in_copies[2:]:
        copy.wait()
    head_rows(
        row_scale, classes, state_ref, head_ref, b1_ref, b2_ref, label_ref,
        state_ref, share_ref, sum1_ref, sum2_ref,
    )
    share_copy.start()
    scaled_ref[...] = jnp.zeros_like(scaled_ref)

    def backward(at, carry):
        n = OPENING - 1 - at
        mask = mask_ref[early + n]
        backward_rows(
            mask, section_weight(w_ref, n, width), n,
            wide_ref, held_ref, left_ref, grads_ref, state_ref, scaled_ref,
        )

        @pl.when(at == OPENING - 1)
        def _():
            for copy in last_copies:
                copy.start()

        @pl.when(at >= 2)
        def _():
            made_copy(at - 2).wait()

        backward_weights(mask, lax.rem(at, 2), left_ref, grads_ref, turned_ref, made_ref)
        made_copy(at).start()
        return carry

    lax.fori_loop(0, OPENING, backward, 0)
    for at in (OPENING - 2, OPENING - 1):
        made_copy(at).wait()
    for copy in [share_copy, *last_copies]:
        copy.wait()


def run_upper(place, masks, b1, b2, labels, weights, state, low, turned, heads, classes):
    rows, width = state.shape
    blocks = weights.shape[0]
    depth = width // blocks
    hidden = b1.shape[1]
    anywhere = pl.BlockSpec(memory_space=pl.ANY)
    inside = pl.BlockSpec(memory_space=pltpu.VMEM)
    tall = jax.ShapeDtypeStruct((rows, width), F32)
    return pl.pallas_call(
        functools.partial(upper_kernel, 1.0 / rows, classes),
        in_specs=[pl.BlockSpec(memory_space=pltpu.SMEM)] + [inside] * 4 + [anywhere] * 6,
        out_specs=[anywhere] * 3 + [inside] * 2,
        out_shape=[
            tall,
            tall,
            jax.ShapeDtypeStruct((blocks, 2, OPENING * depth + HEAD_ROWS, 3 * width), BF16),
            jax.ShapeDtypeStruct((1, hidden), F32),
            jax.ShapeDtypeStruct((1, LANES), F32),
        ],
        scratch_shapes=[
            pltpu.VMEM((OPENING, rows, width), F32),
            pltpu.VMEM((OPENING, 3, rows, width), BF16),
            pltpu.VMEM((OPENING, blocks, 2, depth, 3 * width), BF16),
            pltpu.VMEM((4, 4, 2, HEAD_ROWS, hidden + LANES), BF16),
            pltpu.VMEM((rows, width), BF16),
            pltpu.VMEM((width, rows), BF16),
            pltpu.VMEM((rows, width), F32),
            pltpu.VMEM((rows, width), F32),
            pltpu.VMEM((blocks, 2, HEAD_ROWS, 3 * width), BF16),
            pltpu.VMEM((2, blocks, 2, depth, 3 * width), BF16),
            pltpu.VMEM((2, width, rows), BF16),
            pltpu.VMEM((rows, 3 * width), BF16),
            pltpu.SemaphoreType.DMA((OPENING,)),
            pltpu.SemaphoreType.DMA((2,)),
            pltpu.SemaphoreType.DMA((5,)),
            pltpu.SemaphoreType.DMA((3,)),
        ],
        compiler_params=pltpu.CompilerParams(vmem_limit_bytes=VMEM_LIMIT),
        name="sections_and_head",
    )(place, masks, b1, b2, labels, weights, state, low, turned, *heads)


def lower_kernel(
    total_rows,
    place_ref, mask_ref, x_ref, stat_ref, s_in, u_in, r_in, o_in, weights, turned_in, grad_in, scaled_in,
    own_x, pass_x, total_out, sums_ref,
    wide_ref, held_ref, w_ref, turned_ref, grad_ref, scaled_ref,
    made_ref, left_ref, grads_ref, load_sem, in_sem, made_sem, out_sem,
):
    rows, width = grad_ref.shape
    depth = w_ref.shape[3]
    count = s_in.shape[0]
    core = place_ref[2]
    quarter = own_x.shape[3]

    def load_copies(at):
        n, slot = count - 1 - at, lax.rem(at, 2)
        rows_at = pl.ds(pl.multiple_of(n * depth, depth), depth)
        return [
            pltpu.make_async_copy(s_in.at[n], wide_ref.at[slot], load_sem.at[slot, 0]),
            *[
                pltpu.make_async_copy(array.at[n], held_ref.at[slot, which], load_sem.at[slot, 1 + which])
                for which, array in enumerate((u_in, r_in, o_in))
            ],
            pltpu.make_async_copy(weights.at[:, :, rows_at, :], w_ref.at[slot], load_sem.at[slot, 4]),
        ]

    def column_copies(at, slot):
        rows_at = pl.ds(pl.multiple_of(at * depth, depth), depth)
        return [
            pltpu.make_async_copy(
                made_ref.at[slot, :, side, :, pl.ds(q * quarter, quarter)],
                out.at[q, :, rows_at, :],
                made_sem.at[slot, which, q],
            )
            for which, (side, out) in enumerate(((core, own_x), (1 - core, pass_x)))
            for q in range(4)
        ]

    grad_copy = pltpu.make_async_copy(grad_in, grad_ref, in_sem.at[0])
    scaled_copy = pltpu.make_async_copy(scaled_in, scaled_ref, in_sem.at[1])
    turned_copy = pltpu.make_async_copy(turned_in, turned_ref, in_sem.at[2])
    total_copy = pltpu.make_async_copy(scaled_ref, total_out, out_sem.at[0])
    grad_copy.start()
    for copy in load_copies(0):
        copy.start()
    scaled_copy.start()
    turned_copy.start()
    grad_copy.wait()

    def backward(at, carry):
        n, slot = count - 1 - at, lax.rem(at, 2)
        for copy in load_copies(at):
            copy.wait()

        @pl.when(at == 0)
        def _():
            scaled_copy.wait()

        @pl.when(at + 1 < count)
        def _():
            for copy in load_copies(at + 1):
                copy.start()

        backward_rows(
            mask_ref[n], section_weight(w_ref, slot, width), slot,
            wide_ref, held_ref, left_ref, grads_ref, grad_ref, scaled_ref,
        )

        @pl.when(at == 0)
        def _():
            turned_copy.wait()

        @pl.when(at >= 2)
        def _():
            for copy in column_copies(at - 2, slot):
                copy.wait()

        @pl.when(at == count - 1)
        def _():
            total = scaled_ref[...] + grad_ref[...]
            scaled_ref[...] = total
            normed, _ = normalise(total_rows, x_ref[...], stat_ref[...])
            sums_ref[0:1] = jnp.sum(total, 0, keepdims=True)
            sums_ref[1:2] = jnp.sum(total * normed, 0, keepdims=True)
            total_copy.start()

        backward_weights(mask_ref[n], slot, left_ref, grads_ref, turned_ref, made_ref)

        for copy in column_copies(at, slot):
            copy.start()
        return carry

    lax.fori_loop(0, count, backward, 0)
    for at in range(max(count - 2, 0), count):
        for copy in column_copies(at, at % 2):
            copy.wait()
    total_copy.wait()


def run_lower(place, masks, features, stats, saved, weights, turned, grad_state, grad_scaled, total_rows):
    rows, width = features.shape
    blocks = weights.shape[0]
    depth = width // blocks
    count = saved[0].shape[0]
    columns = 3 * width
    anywhere = pl.BlockSpec(memory_space=pl.ANY)
    inside = pl.BlockSpec(memory_space=pltpu.VMEM)
    across = jax.ShapeDtypeStruct((4, blocks, count * depth, columns // 4), BF16)
    return pl.pallas_call(
        functools.partial(lower_kernel, total_rows),
        in_specs=[pl.BlockSpec(memory_space=pltpu.SMEM)] + [inside] * 3 + [anywhere] * 8,
        out_specs=[anywhere] * 3 + [inside],
        out_shape=[
            across,
            across,
            jax.ShapeDtypeStruct((rows, width), F32),
            jax.ShapeDtypeStruct((2, width), F32),
        ],
        scratch_shapes=[
            pltpu.VMEM((2, rows, width), F32),
            pltpu.VMEM((2, 3, rows, width), BF16),
            pltpu.VMEM((2, blocks, 2, depth, columns), BF16),
            pltpu.VMEM((width, rows), BF16),
            pltpu.VMEM((rows, width), F32),
            pltpu.VMEM((rows, width), F32),
            pltpu.VMEM((2, blocks, 2, depth, columns), BF16),
            pltpu.VMEM((2, width, rows), BF16),
            pltpu.VMEM((rows, columns), BF16),
            pltpu.SemaphoreType.DMA((2, 5)),
            pltpu.SemaphoreType.DMA((3,)),
            pltpu.SemaphoreType.DMA((2, 2, 4)),
            pltpu.SemaphoreType.DMA((1,)),
        ],
        compiler_params=pltpu.CompilerParams(vmem_limit_bytes=VMEM_LIMIT),
        name="sections_backward",
    )(place, masks, features, stats, *saved, weights, turned, grad_state, grad_scaled)


def pairs(sizes, axis, flip):
    table = []
    for source in range(math.prod(sizes)):
        place = list(np.unravel_index(source, sizes))
        place[axis] ^= flip
        table.append((source, int(np.ravel_multi_index(place, sizes))))
    return table


def everywhere_sum(value, sizes, names, axes=(3, 2, 1, 0)):
    for axis in axes:
        for flip in (1, 3) if sizes[axis] == 4 else (1,):
            value = value + lax.ppermute(value, names, pairs(sizes, axis, flip))
    return value


def add(*parts):
    return functools.reduce(lambda a, b: a + b, [part.astype(F32) for part in parts])


def shifted(sizes, axis, by):
    table = []
    for source in range(math.prod(sizes)):
        place = list(np.unravel_index(source, sizes))
        place[axis] = (place[axis] + by) % sizes[axis]
        table.append((source, int(np.ravel_multi_index(place, sizes))))
    return table


def in_order(parts, at):
    turned = jnp.stack(parts[::-1] * 2, 0)
    return lax.dynamic_slice_in_dim(turned, 3 - at, 4, 0)


def core_groups(count):
    return [[2 * at + core for at in range(count)] for core in range(2)]


def quarter_gather(shard, head, stats, also, sizes, names, place):
    send = lambda value, axis, by: lax.ppermute(value, names, shifted(sizes, axis, by))
    quarter = shard.shape[1] // 4
    own = lax.dynamic_slice_in_dim(shard, place[3] * quarter, quarter, 1)
    own = jnp.concatenate([own, head], 0)
    count = sizes[1] * sizes[2]
    plane = lax.all_to_all(
        jnp.broadcast_to(own[None], (count, *own.shape)), "fsdp", 0, 0,
        axis_index_groups=core_groups(count),
    )
    plane = plane.reshape(sizes[1], sizes[2], *own.shape)
    stats = everywhere_sum(stats, sizes, names, (3, 0))
    plane, stats, also = lax.optimization_barrier((plane, stats, also))
    moved = plane[:, :, : shard.shape[0]]
    behind, ahead = send(moved, 0, 1), send(moved, 0, 3)
    stats = everywhere_sum(stats, sizes, names, (2, 1))
    behind, ahead, stats = lax.optimization_barrier((behind, ahead, stats))
    arrived = [plane, behind, ahead, send(behind[:2], 0, 1), send(ahead[2:], 0, 3)]
    pieces = []
    for piece in arrived:
        pieces += [piece, lax.ppermute(piece, names, pairs(sizes, 3, 1))]
    return pieces, stats, also


def column_scatter(total):
    got = lax.all_to_all(total, "dp", 0, 0)
    return jnp.sum(got.astype(F32), 0).astype(BF16)


def plane_scatter(total):
    got = lax.all_to_all(
        total, "fsdp", 0, 0, axis_index_groups=core_groups(total.shape[0])
    )
    return jnp.sum(got.astype(F32), 0).astype(BF16)


def column_gather(part, sizes, names, place):
    parts = [part] + [lax.ppermute(part, names, shifted(sizes, 0, by)) for by in (1, 2, 3)]
    return jnp.concatenate(list(in_order(parts, place[3])), 1).astype(F32)


def column_sum(value, sizes, names, flips=(1, 3)):
    for flip in flips:
        other = lax.ppermute(value, names, pairs(sizes, 0, flip))
        value = add(value, other)
        if flip == flips[0]:
            value = value.astype(BF16)
    return value


def on_device(
    sizes,
    features,
    bn_gain,
    bn_bias,
    gate_weights,
    feature_masks,
    head_first,
    head_first_bias,
    head_second,
    head_second_bias,
    labels,
):
    names = ("dp", "fsdp")
    rows, width = features.shape
    sections, depth, columns = gate_weights.shape
    hidden = head_first.shape[1]
    classes = head_second.shape[1]
    total_rows = rows * math.prod(sizes)
    gain, bias = bn_gain[None], bn_bias[None]
    masks = feature_masks.astype(F32)[:, None, :]
    b1 = head_first_bias[None]
    b2 = jnp.pad(head_second_bias, (0, LANES - classes))[None]

    inputs = features.astype(F32)
    stats = jnp.stack([jnp.sum(inputs, 0), jnp.sum(inputs * inputs, 0)])
    early = sections - OPENING
    late = gate_weights[early:].reshape(OPENING * depth, columns)
    weights = lax.all_gather(late, "fsdp", axis=0)
    weights = weights.reshape(-1, 2, *weights.shape[1:])
    extra = jnp.pad(head_first, ((0, 0), (0, LANES))) + jnp.pad(
        head_second, ((0, HEAD_ROWS - head_second.shape[0]), (hidden, LANES - classes))
    )
    fsdp = lax.axis_index("fsdp")
    place = jnp.stack([fsdp // 8, fsdp // 2 % 4, fsdp % 2, lax.axis_index("dp")])
    pieces, stats, also = quarter_gather(
        gate_weights[:early].reshape(early * depth, columns), extra,
        stats.reshape(-1, LANES), (masks, b2, place, labels[:, None]), sizes, names, place,
    )
    masks, b2, place, labels = also
    stats = stats.reshape(2, width)
    *saved, state, low, turned, full = run_entry(
        place, features, stats, gain, bias, masks, pieces, early, total_rows
    )
    full = full.reshape(16, 2, early * depth, columns)
    grad_state, grad_scaled, top, sum1, sum2 = run_upper(
        place, masks, b1, b2, labels, weights, state, low, turned, pieces[:2], classes
    )
    top = lax.psum_scatter(top.reshape(-1, *top.shape[2:]), "fsdp", scatter_dimension=0)
    own_x, pass_x, grad_scaled, *sums = run_lower(
        place, masks, features, stats, saved, full, turned, grad_state, grad_scaled, total_rows
    )
    across = add(own_x, lax.ppermute(pass_x, names, pairs(sizes, 3, 1))).astype(BF16)
    across, sums = lax.optimization_barrier((across, sums))
    across = column_scatter(across)
    small = jnp.concatenate([sums[0].reshape(-1), sum1[0], sum2[0]])
    small = jnp.pad(small, (0, -small.size % 1024)).reshape(-1, LANES)
    small = everywhere_sum(small, sizes, names, (3, 2))
    small, across = lax.optimization_barrier((small, across))
    across = plane_scatter(across)
    small = everywhere_sum(small, sizes, names, (1, 0))
    small, across = lax.optimization_barrier((small, across))
    across = column_gather(across, sizes, names, place)
    small, top, across = lax.optimization_barrier((small, top, across))
    small = small.reshape(-1)
    cut = top.shape[0] // 32 * 16
    top = jnp.concatenate(
        [
            column_sum(top[:cut], sizes, names),
            column_sum(top[cut:], sizes, names, (3, 1)),
        ],
        0,
    )
    finished = [None] * sections
    order = list(range(sections))[::-1]
    for part, start, stop in ((top, 0, OPENING), (across, OPENING, sections)):
        for at, n in enumerate(order[start:stop]):
            finished[n] = part[at * depth : (at + 1) * depth]
    head_grad = top[OPENING * depth :]
    gate_grad = jnp.stack(finished, 0)
    head_first_grad = head_grad[:, :hidden]
    head_second_grad = head_grad[: head_second.shape[0], hidden : hidden + classes]

    sum_grad, sum_cross = small[:width], small[width : 2 * width]
    first_bias_grad = small[2 * width : 2 * width + hidden]
    second_bias_grad = small[2 * width + hidden : 2 * width + hidden + classes]
    normed, scale = normalise(total_rows, features, stats)
    features_grad = (
        scale * gain * (grad_scaled - sum_grad / total_rows - normed * (sum_cross / total_rows))
    )
    return (
        features_grad,
        sum_cross,
        sum_grad,
        gate_grad,
        head_first_grad,
        first_bias_grad,
        head_second_grad,
        second_bias_grad,
    )


def solution(mesh):
    placed = (
        P(("dp", "fsdp"), None),
        P(),
        P(),
        P(None, "fsdp", None),
        P(),
        P("fsdp", None),
        P(),
        P("fsdp", None),
        P(),
        P(("dp", "fsdp")),
    )
    sizes = (mesh.shape["dp"], 4, 4, mesh.shape["fsdp"] // 16)
    return jax.shard_map(
        functools.partial(on_device, sizes),
        mesh=mesh,
        in_specs=placed,
        out_specs=(
            P(("dp", "fsdp"), None),
            P(),
            P(),
            P(None, "fsdp", None),
            P("fsdp", None),
            P(),
            P("fsdp", None),
            P(),
        ),
        check_vma=False,
    )
```

```python
import functools
import math

import jax
import jax.numpy as jnp
import numpy as np
from jax import lax
from jax.experimental import pallas as pl
from jax.experimental.pallas import tpu as pltpu
from jax.sharding import PartitionSpec as P

epsilon = 1e-05
F32 = jnp.float32
BF16 = jnp.bfloat16
MIB = 1024 * 1024
HEAD_ROWS = 16
OPENING = 4
QUARTERS = ((0, 0, 4), (1, 0, 4), (3, 0, 4), (2, 0, 2), (2, 2, 4))
PIECES = 2 * len(QUARTERS)
LANES = 128


def sigmoid(value):
    return 0.5 * jnp.tanh(0.5 * value) + 0.5


def dot(left, right):
    return jnp.dot(left, right, preferred_element_type=F32)


def dot_cols(left, right):
    return lax.dot_general(left, right, (((1,), (1,)), ((), ())), preferred_element_type=F32)


def erf(value):
    value = jnp.clip(value, -4.0, 4.0)
    square = value * value
    top = jnp.full_like(square, -2.72614225801306e-10)
    for term in (
        2.77068142495902e-08,
        -2.10102402082508e-06,
        -5.69250639462346e-05,
        -7.34990630326855e-04,
        -2.95459980854025e-03,
        -1.60960333262415e-02,
    ):
        top = top * square + term
    low = jnp.full_like(square, -1.45660718464996e-05)
    for term in (
        -2.13374055278905e-04,
        -1.68282697438203e-03,
        -7.37332916720468e-03,
        -1.42647390514189e-02,
    ):
        low = low * square + term
    return value * top / low


def normalise(total_rows, features, stats):
    mean = stats[0:1] / total_rows
    scale = lax.rsqrt(stats[1:2] / total_rows - mean * mean + epsilon)
    return (features.astype(F32) - mean) * scale, scale


def halves(rows):
    return [slice(0, rows // 2), slice(rows // 2, rows)]


def section_weight(w_ref, slot, width):
    half = w_ref.shape[1] // 2

    def weight(lower, start):
        place = slice(0, half) if lower else slice(half, 2 * half)
        return w_ref[slot, place, ..., start : start + width].reshape(width, width)

    return weight


def forward_section(mask, weight, slot, wide_ref, held_ref, state_ref, low_ref):
    rows, width = state_ref.shape
    mask = mask.astype(BF16)
    for part in halves(rows):
        state = state_ref[part]
        state_low = state.astype(BF16)
        masked = low_ref[part] * mask
        wide_ref[slot, part] = state
        reset = sigmoid(dot(state_low, weight(True, width)) + dot(masked, weight(False, width)))
        held_ref[slot, 1, part] = reset.astype(BF16)
        second = (reset * state).astype(BF16)
        update = sigmoid(dot(state_low, weight(True, 0)) + dot(masked, weight(False, 0)))
        held_ref[slot, 0, part] = update.astype(BF16)
        output = jnp.tanh(
            dot(second, weight(True, 2 * width)) + dot(masked, weight(False, 2 * width))
        )
        held_ref[slot, 2, part] = output.astype(BF16)
        state_ref[part] = state + update * (output - state)


def backward_rows(mask, weight, slot, wide_ref, held_ref, left_ref, grads_ref, grad_ref, scaled_ref):
    rows, width = grad_ref.shape
    for part in halves(rows):
        grad = grad_ref[part]
        state = wide_ref[slot, part]
        update, reset, output = [held_ref[slot, which, part].astype(F32) for which in range(3)]
        left_ref[0, :, part] = state.astype(BF16).T
        left_ref[1, :, part] = (reset * state).astype(BF16).T
        grad_output = (grad * update * (1.0 - output * output)).astype(BF16)
        grads_ref[part, 2 * width :] = grad_output
        grad_update = (grad * (output - state) * update * (1.0 - update)).astype(BF16)
        grads_ref[part, 0:width] = grad_update
        through = dot_cols(grad_output, weight(True, 2 * width))
        grad_reset = (through * state * reset * (1.0 - reset)).astype(BF16)
        grads_ref[part, width : 2 * width] = grad_reset
        grad_ref[part] = (
            grad * (1.0 - update)
            + through * reset
            + dot_cols(grad_update, weight(True, 0))
            + dot_cols(grad_reset, weight(True, width))
        )
        scaled_ref[part] += mask * (
            dot_cols(grad_update, weight(False, 0))
            + dot_cols(grad_reset, weight(False, width))
            + dot_cols(grad_output, weight(False, 2 * width))
        )


def backward_weights(mask, slot, left_ref, grads_ref, turned_ref, made_ref):
    width = turned_ref.shape[0]
    blocks, depth = made_ref.shape[1], made_ref.shape[3]
    column = jnp.broadcast_to(mask, (8, width)).T[:, 0:1]

    def put(place, columns, value):
        value = value.astype(BF16).reshape(blocks // 2, 2, depth, width)
        made_ref[slot, place, :, :, columns] = value

    for gate in range(3):
        columns = slice(gate * width, (gate + 1) * width)
        put(slice(0, blocks // 2), columns, dot(left_ref[gate // 2], grads_ref[:, columns]))
        put(
            slice(blocks // 2, blocks),
            columns,
            column * dot(turned_ref[...], grads_ref[:, columns]),
        )


def head_rows(
    row_scale, classes, state_ref, head_ref, b1_ref, b2_ref, label_ref,
    grad_ref, share_ref, sum1_ref, sum2_ref,
):
    rows, width = state_ref.shape
    blocks = share_ref.shape[0]
    owners = 2 * blocks
    hidden = b1_ref.shape[1]
    first = head_ref[..., 0:hidden].reshape(width, hidden)
    second = head_ref[..., hidden : hidden + LANES].astype(F32)[..., 0 : hidden // owners, :]
    second = second.reshape(hidden, LANES).astype(BF16)
    head_in = state_ref[...].astype(BF16)
    pre = dot(head_in, first) + b1_ref[...]
    phi = 0.5 + 0.5 * erf(pre * math.sqrt(0.5))
    activation = (pre * phi).astype(BF16)
    slope = phi + pre * (jnp.exp(-0.5 * pre * pre) * (1.0 / math.sqrt(2.0 * math.pi)))
    lane = lax.broadcasted_iota(jnp.int32, (rows, LANES), 1)
    logits = dot(activation, second) + b2_ref[...]
    logits = jnp.where(lane < classes, logits, -1e30)
    powers = jnp.exp(logits - jnp.max(logits, 1, keepdims=True))
    chance = powers / jnp.sum(powers, 1, keepdims=True)
    hit = jnp.where(lane == label_ref[...], 1.0, 0.0)
    grad_logits = ((chance - hit) * row_scale).astype(BF16)
    sum2_ref[...] = jnp.sum(grad_logits.astype(F32), 0, keepdims=True)
    grad_second = dot(activation.T, grad_logits)
    grad_pre = (dot_cols(grad_logits, second) * slope).astype(BF16)
    sum1_ref[...] = jnp.sum(grad_pre.astype(F32), 0, keepdims=True)
    grad_first = dot(head_in.T, grad_pre)
    grad_ref[...] = dot_cols(grad_pre, first)
    grad_second = grad_second.reshape(blocks, 2, hidden // owners, LANES)
    grad_second = jnp.concatenate([grad_second, jnp.zeros_like(grad_second)], 2)
    share_ref[:, :, :, 0:hidden] = grad_first.reshape(blocks, 2, HEAD_ROWS, hidden).astype(BF16)
    share_ref[:, :, :, hidden : hidden + LANES] = grad_second.astype(BF16)
    tail = share_ref.shape[3] - hidden - LANES
    share_ref[:, :, :, hidden + LANES :] = jnp.zeros((blocks, 2, HEAD_ROWS, tail), BF16)


def entry_kernel(
    total_rows, place_ref, x_ref, stat_ref, gain_ref, bias_ref, mask_ref, *refs,
):
    pieces, refs = refs[:PIECES], refs[PIECES:]
    s_out, u_out, r_out, o_out, state_out, low_out, turned_out, full_out = refs[:8]
    wide_ref, held_ref, w_ref, low_ref, turned_ref, state_ref, w_sem, save_sem, out_sem = refs[8:]
    rows, width = x_ref.shape
    count, depth = w_ref.shape[0], w_ref.shape[4]
    quarter = w_ref.shape[5] // 4

    def piece_copies(at):
        copies = []
        for which, piece in enumerate(pieces):
            (by, first, last), side = QUARTERS[which // 2], which % 2
            core = place_ref[2] if side == 0 else 1 - place_ref[2]
            start = pl.multiple_of(lax.rem(place_ref[3] + 4 - by, 4) * quarter, LANES)
            copies.append(
                pltpu.make_async_copy(
                    piece.at[:, :, pl.ds(at * depth, depth)],
                    w_ref.at[at, first:last, :, core, :, pl.ds(start, quarter)],
                    w_sem.at[at, which],
                )
            )
        return copies

    def save_copies(at):
        return [
            pltpu.make_async_copy(w_ref.at[at], full_out.at[:, :, :, at], save_sem.at[at, 0]),
            pltpu.make_async_copy(wide_ref.at[at], s_out.at[at], save_sem.at[at, 1]),
        ] + [
            pltpu.make_async_copy(held_ref.at[at, which], out.at[at], save_sem.at[at, which + 2])
            for which, out in enumerate((u_out, r_out, o_out))
        ]

    out_copies = [
        pltpu.make_async_copy(low_ref, low_out, out_sem.at[0]),
        pltpu.make_async_copy(turned_ref, turned_out, out_sem.at[1]),
        pltpu.make_async_copy(state_ref, state_out, out_sem.at[2]),
    ]
    for at in range(count):
        for copy in piece_copies(at):
            copy.start()
    for part in halves(rows):
        normed, _ = normalise(total_rows, x_ref[part], stat_ref[...])
        scaled = normed * gain_ref[...] + bias_ref[...]
        state_ref[part] = scaled
        low = scaled.astype(BF16)
        low_ref[part] = low
        turned_ref[:, part] = low.T
    for copy in out_copies[:2]:
        copy.start()
    for at in range(count):
        for copy in piece_copies(at):
            copy.wait()
        forward_section(
            mask_ref[at], section_weight(w_ref, at, width), at,
            wide_ref, held_ref, state_ref, low_ref,
        )
        for copy in save_copies(at):
            copy.start()
    out_copies[2].start()
    for at in range(count):
        for copy in save_copies(at):
            copy.wait()
    for copy in out_copies:
        copy.wait()


def run_entry(place, features, stats, gain, bias, masks, pieces, count, total_rows):
    rows, width = features.shape
    depth = pieces[2].shape[2] // count
    anywhere = pl.BlockSpec(memory_space=pl.ANY)
    inside = pl.BlockSpec(memory_space=pltpu.VMEM)
    return pl.pallas_call(
        functools.partial(entry_kernel, total_rows),
        in_specs=[pl.BlockSpec(memory_space=pltpu.SMEM)] + [inside] * 5 + [anywhere] * PIECES,
        out_specs=[pl.BlockSpec(memory_space=pltpu.HBM)] * 8,
        out_shape=[
            jax.ShapeDtypeStruct((count, rows, width), kind) for kind in (F32, BF16, BF16, BF16)
        ]
        + [
            jax.ShapeDtypeStruct((rows, width), F32),
            jax.ShapeDtypeStruct((rows, width), BF16),
            jax.ShapeDtypeStruct((width, rows), BF16),
            jax.ShapeDtypeStruct((4, 4, 2, count, depth, 3 * width), BF16),
        ],
        scratch_shapes=[
            pltpu.VMEM((count, rows, width), F32),
            pltpu.VMEM((count, 3, rows, width), BF16),
            pltpu.VMEM((count, 4, 4, 2, depth, 3 * width), BF16),
            pltpu.VMEM((rows, width), BF16),
            pltpu.VMEM((width, rows), BF16),
            pltpu.VMEM((rows, width), F32),
            pltpu.SemaphoreType.DMA((count, PIECES)),
            pltpu.SemaphoreType.DMA((count, 5)),
            pltpu.SemaphoreType.DMA((3,)),
        ],
        compiler_params=pltpu.CompilerParams(vmem_limit_bytes=55 * MIB),
        name="first_sections",
    )(place, features, stats, gain, bias, masks, *pieces)


def upper_kernel(
    row_scale, classes,
    place_ref, mask_ref, b1_ref, b2_ref, label_ref, weights, state_in, low_in, turned_in, head_own, head_other,
    grad_out, scaled_out, made_out, sum1_ref, sum2_ref,
    wide_ref, held_ref, w_ref, head_ref, low_ref, turned_ref, state_ref, scaled_ref,
    share_ref, made_ref, left_ref, grads_ref, w_sem, made_sem, in_sem, out_sem,
):
    rows, width = state_ref.shape
    depth = w_ref.shape[3]
    early = mask_ref.shape[0] - OPENING

    def w_copy(n):
        rows_at = pl.ds(pl.multiple_of(n * depth, depth), depth)
        return pltpu.make_async_copy(weights.at[:, :, rows_at, :], w_ref.at[n], w_sem.at[n])

    def made_copy(at):
        rows_at = pl.ds(pl.multiple_of(at * depth, depth), depth)
        slot = lax.rem(at, 2)
        return pltpu.make_async_copy(
            made_ref.at[slot], made_out.at[:, :, rows_at, :], made_sem.at[slot]
        )

    head_rows_at = pl.ds(head_own.shape[2] - HEAD_ROWS, HEAD_ROWS)
    in_copies = [
        pltpu.make_async_copy(state_in, state_ref, in_sem.at[0]),
        pltpu.make_async_copy(low_in, low_ref, in_sem.at[1]),
        pltpu.make_async_copy(turned_in, turned_ref, in_sem.at[2]),
    ] + [
        pltpu.make_async_copy(
            array.at[:, :, head_rows_at], head_ref.at[:, :, side], in_sem.at[3 + which]
        )
        for which, (array, side) in enumerate(
            ((head_own, place_ref[2]), (head_other, 1 - place_ref[2]))
        )
    ]
    share_copy = pltpu.make_async_copy(
        share_ref, made_out.at[:, :, pl.ds(OPENING * depth, HEAD_ROWS), :], out_sem.at[0]
    )
    last_copies = [
        pltpu.make_async_copy(state_ref, grad_out, out_sem.at[1]),
        pltpu.make_async_copy(scaled_ref, scaled_out, out_sem.at[2]),
    ]
    for copy in in_copies[:2]:
        copy.start()
    w_copy(0).start()
    w_copy(1).start()
    for copy in in_copies[2:]:
        copy.start()
    for copy in in_copies[:2]:
        copy.wait()

    def forward(n, carry):
        w_copy(n).wait()

        @pl.when((n >= 1) & (n + 1 < OPENING))
        def _():
            w_copy(n + 1).start()

        forward_section(
            mask_ref[early + n], section_weight(w_ref, n, width), n,
            wide_ref, held_ref, state_ref, low_ref,
        )
        return carry

    lax.fori_loop(0, OPENING, forward, 0)
    for copy in in_copies[2:]:
        copy.wait()
    head_rows(
        row_scale, classes, state_ref, head_ref, b1_ref, b2_ref, label_ref,
        state_ref, share_ref, sum1_ref, sum2_ref,
    )
    share_copy.start()
    scaled_ref[...] = jnp.zeros_like(scaled_ref)

    def backward(at, carry):
        n = OPENING - 1 - at
        mask = mask_ref[early + n]
        backward_rows(
            mask, section_weight(w_ref, n, width), n,
            wide_ref, held_ref, left_ref, grads_ref, state_ref, scaled_ref,
        )

        @pl.when(at == OPENING - 1)
        def _():
            for copy in last_copies:
                copy.start()

        @pl.when(at >= 2)
        def _():
            made_copy(at - 2).wait()

        backward_weights(mask, lax.rem(at, 2), left_ref, grads_ref, turned_ref, made_ref)
        made_copy(at).start()
        return carry

    lax.fori_loop(0, OPENING, backward, 0)
    for at in (OPENING - 2, OPENING - 1):
        made_copy(at).wait()
    for copy in [share_copy, *last_copies]:
        copy.wait()


def run_upper(place, masks, b1, b2, labels, weights, state, low, turned, heads, classes):
    rows, width = state.shape
    blocks = weights.shape[0]
    depth = width // blocks
    hidden = b1.shape[1]
    anywhere = pl.BlockSpec(memory_space=pl.ANY)
    inside = pl.BlockSpec(memory_space=pltpu.VMEM)
    tall = jax.ShapeDtypeStruct((rows, width), F32)
    return pl.pallas_call(
        functools.partial(upper_kernel, 1.0 / rows, classes),
        in_specs=[pl.BlockSpec(memory_space=pltpu.SMEM)] + [inside] * 4 + [anywhere] * 6,
        out_specs=[anywhere] * 3 + [inside] * 2,
        out_shape=[
            tall,
            tall,
            jax.ShapeDtypeStruct((blocks, 2, OPENING * depth + HEAD_ROWS, 3 * width), BF16),
            jax.ShapeDtypeStruct((1, hidden), F32),
            jax.ShapeDtypeStruct((1, LANES), F32),
        ],
        scratch_shapes=[
            pltpu.VMEM((OPENING, rows, width), F32),
            pltpu.VMEM((OPENING, 3, rows, width), BF16),
            pltpu.VMEM((OPENING, blocks, 2, depth, 3 * width), BF16),
            pltpu.VMEM((4, 4, 2, HEAD_ROWS, hidden + LANES), BF16),
            pltpu.VMEM((rows, width), BF16),
            pltpu.VMEM((width, rows), BF16),
            pltpu.VMEM((rows, width), F32),
            pltpu.VMEM((rows, width), F32),
            pltpu.VMEM((blocks, 2, HEAD_ROWS, 3 * width), BF16),
            pltpu.VMEM((2, blocks, 2, depth, 3 * width), BF16),
            pltpu.VMEM((2, width, rows), BF16),
            pltpu.VMEM((rows, 3 * width), BF16),
            pltpu.SemaphoreType.DMA((OPENING,)),
            pltpu.SemaphoreType.DMA((2,)),
            pltpu.SemaphoreType.DMA((5,)),
            pltpu.SemaphoreType.DMA((3,)),
        ],
        compiler_params=pltpu.CompilerParams(vmem_limit_bytes=60 * MIB),
        name="sections_and_head",
    )(place, masks, b1, b2, labels, weights, state, low, turned, *heads)


def lower_kernel(
    total_rows,
    place_ref, mask_ref, x_ref, stat_ref, s_in, u_in, r_in, o_in, weights, turned_in, grad_in, scaled_in,
    own_x, pass_x, total_out, sums_ref,
    wide_ref, held_ref, w_ref, turned_ref, grad_ref, scaled_ref,
    made_ref, left_ref, grads_ref, load_sem, in_sem, made_sem, out_sem,
):
    rows, width = grad_ref.shape
    depth = w_ref.shape[3]
    count = s_in.shape[0]
    core = place_ref[2]
    quarter = own_x.shape[3]

    def load_copies(at):
        n, slot = count - 1 - at, lax.rem(at, 2)
        rows_at = pl.ds(pl.multiple_of(n * depth, depth), depth)
        return [
            pltpu.make_async_copy(s_in.at[n], wide_ref.at[slot], load_sem.at[slot, 0]),
            *[
                pltpu.make_async_copy(array.at[n], held_ref.at[slot, which], load_sem.at[slot, 1 + which])
                for which, array in enumerate((u_in, r_in, o_in))
            ],
            pltpu.make_async_copy(weights.at[:, :, rows_at, :], w_ref.at[slot], load_sem.at[slot, 4]),
        ]

    def column_copies(at, slot):
        rows_at = pl.ds(pl.multiple_of(at * depth, depth), depth)
        return [
            pltpu.make_async_copy(
                made_ref.at[slot, :, side, :, pl.ds(q * quarter, quarter)],
                out.at[q, :, rows_at, :],
                made_sem.at[slot, which, q],
            )
            for which, (side, out) in enumerate(((core, own_x), (1 - core, pass_x)))
            for q in range(4)
        ]

    grad_copy = pltpu.make_async_copy(grad_in, grad_ref, in_sem.at[0])
    scaled_copy = pltpu.make_async_copy(scaled_in, scaled_ref, in_sem.at[1])
    turned_copy = pltpu.make_async_copy(turned_in, turned_ref, in_sem.at[2])
    total_copy = pltpu.make_async_copy(scaled_ref, total_out, out_sem.at[0])
    grad_copy.start()
    for copy in load_copies(0):
        copy.start()
    scaled_copy.start()
    turned_copy.start()
    grad_copy.wait()

    def backward(at, carry):
        n, slot = count - 1 - at, lax.rem(at, 2)
        for copy in load_copies(at):
            copy.wait()

        @pl.when(at == 0)
        def _():
            scaled_copy.wait()

        @pl.when(at + 1 < count)
        def _():
            for copy in load_copies(at + 1):
                copy.start()

        backward_rows(
            mask_ref[n], section_weight(w_ref, slot, width), slot,
            wide_ref, held_ref, left_ref, grads_ref, grad_ref, scaled_ref,
        )

        @pl.when(at == 0)
        def _():
            turned_copy.wait()

        @pl.when(at >= 2)
        def _():
            for copy in column_copies(at - 2, slot):
                copy.wait()

        @pl.when(at == count - 1)
        def _():
            total = scaled_ref[...] + grad_ref[...]
            scaled_ref[...] = total
            normed, _ = normalise(total_rows, x_ref[...], stat_ref[...])
            sums_ref[0:1] = jnp.sum(total, 0, keepdims=True)
            sums_ref[1:2] = jnp.sum(total * normed, 0, keepdims=True)
            total_copy.start()

        backward_weights(mask_ref[n], slot, left_ref, grads_ref, turned_ref, made_ref)

        for copy in column_copies(at, slot):
            copy.start()
        return carry

    lax.fori_loop(0, count, backward, 0)
    for at in range(max(count - 2, 0), count):
        for copy in column_copies(at, at % 2):
            copy.wait()
    total_copy.wait()


def run_lower(place, masks, features, stats, saved, weights, turned, grad_state, grad_scaled, total_rows):
    rows, width = features.shape
    blocks = weights.shape[0]
    depth = width // blocks
    count = saved[0].shape[0]
    columns = 3 * width
    anywhere = pl.BlockSpec(memory_space=pl.ANY)
    inside = pl.BlockSpec(memory_space=pltpu.VMEM)
    across = jax.ShapeDtypeStruct((4, blocks, count * depth, columns // 4), BF16)
    return pl.pallas_call(
        functools.partial(lower_kernel, total_rows),
        in_specs=[pl.BlockSpec(memory_space=pltpu.SMEM)] + [inside] * 3 + [anywhere] * 8,
        out_specs=[anywhere] * 3 + [inside],
        out_shape=[
            across,
            across,
            jax.ShapeDtypeStruct((rows, width), F32),
            jax.ShapeDtypeStruct((2, width), F32),
        ],
        scratch_shapes=[
            pltpu.VMEM((2, rows, width), F32),
            pltpu.VMEM((2, 3, rows, width), BF16),
            pltpu.VMEM((2, blocks, 2, depth, columns), BF16),
            pltpu.VMEM((width, rows), BF16),
            pltpu.VMEM((rows, width), F32),
            pltpu.VMEM((rows, width), F32),
            pltpu.VMEM((2, blocks, 2, depth, columns), BF16),
            pltpu.VMEM((2, width, rows), BF16),
            pltpu.VMEM((rows, columns), BF16),
            pltpu.SemaphoreType.DMA((2, 5)),
            pltpu.SemaphoreType.DMA((3,)),
            pltpu.SemaphoreType.DMA((2, 2, 4)),
            pltpu.SemaphoreType.DMA((1,)),
        ],
        compiler_params=pltpu.CompilerParams(vmem_limit_bytes=60 * MIB),
        name="sections_backward",
    )(place, masks, features, stats, *saved, weights, turned, grad_state, grad_scaled)


def pairs(sizes, axis, flip):
    table = []
    for source in range(math.prod(sizes)):
        place = list(np.unravel_index(source, sizes))
        place[axis] ^= flip
        table.append((source, int(np.ravel_multi_index(place, sizes))))
    return table


def everywhere_sum(value, sizes, names, axes=(3, 2, 1, 0)):
    for axis in axes:
        for flip in (1, 3) if sizes[axis] == 4 else (1,):
            value = value + lax.ppermute(value, names, pairs(sizes, axis, flip))
    return value


def add(*parts):
    return functools.reduce(lambda a, b: a + b, [part.astype(F32) for part in parts])


def shifted(sizes, axis, by):
    table = []
    for source in range(math.prod(sizes)):
        place = list(np.unravel_index(source, sizes))
        place[axis] = (place[axis] + by) % sizes[axis]
        table.append((source, int(np.ravel_multi_index(place, sizes))))
    return table


def in_order(parts, at):
    turned = jnp.stack(parts[::-1] * 2, 0)
    return lax.dynamic_slice_in_dim(turned, 3 - at, 4, 0)


def core_groups(count):
    return [[2 * at + core for at in range(count)] for core in range(2)]


def quarter_gather(shard, head, stats, also, sizes, names, place):
    send = lambda value, axis, by: lax.ppermute(value, names, shifted(sizes, axis, by))
    quarter = shard.shape[1] // 4
    own = lax.dynamic_slice_in_dim(shard, place[3] * quarter, quarter, 1)
    own = jnp.concatenate([own, head], 0)
    count = sizes[1] * sizes[2]
    plane = lax.all_to_all(
        jnp.broadcast_to(own[None], (count, *own.shape)), "fsdp", 0, 0,
        axis_index_groups=core_groups(count),
    )
    plane = plane.reshape(sizes[1], sizes[2], *own.shape)
    stats = everywhere_sum(stats, sizes, names, (3, 0))
    plane, stats, also = lax.optimization_barrier((plane, stats, also))
    moved = plane[:, :, : shard.shape[0]]
    behind, ahead = send(moved, 0, 1), send(moved, 0, 3)
    stats = everywhere_sum(stats, sizes, names, (2, 1))
    behind, ahead, stats = lax.optimization_barrier((behind, ahead, stats))
    arrived = [plane, behind, ahead, send(behind[:2], 0, 1), send(ahead[2:], 0, 3)]
    pieces = []
    for piece in arrived:
        pieces += [piece, lax.ppermute(piece, names, pairs(sizes, 3, 1))]
    return pieces, stats, also


def column_scatter(total):
    got = lax.all_to_all(total, "dp", 0, 0)
    return jnp.sum(got.astype(F32), 0).astype(BF16)


def plane_scatter(total):
    got = lax.all_to_all(
        total, "fsdp", 0, 0, axis_index_groups=core_groups(total.shape[0])
    )
    return jnp.sum(got.astype(F32), 0).astype(BF16)


def column_gather(part, sizes, names, place):
    parts = [part] + [lax.ppermute(part, names, shifted(sizes, 0, by)) for by in (1, 2, 3)]
    return jnp.concatenate(list(in_order(parts, place[3])), 1).astype(F32)


def column_sum(value, sizes, names, flips=(1, 3)):
    for flip in flips:
        other = lax.ppermute(value, names, pairs(sizes, 0, flip))
        value = add(value, other)
        if flip == flips[0]:
            value = value.astype(BF16)
    return value


def on_device(
    sizes,
    features,
    bn_gain,
    bn_bias,
    gate_weights,
    feature_masks,
    head_first,
    head_first_bias,
    head_second,
    head_second_bias,
    labels,
):
    names = ("dp", "fsdp")
    rows, width = features.shape
    sections, depth, columns = gate_weights.shape
    hidden = head_first.shape[1]
    classes = head_second.shape[1]
    total_rows = rows * math.prod(sizes)
    gain, bias = bn_gain[None], bn_bias[None]
    masks = feature_masks.astype(F32)[:, None, :]
    b1 = head_first_bias[None]
    b2 = jnp.pad(head_second_bias, (0, LANES - classes))[None]

    inputs = features.astype(F32)
    stats = jnp.stack([jnp.sum(inputs, 0), jnp.sum(inputs * inputs, 0)])
    early = sections - OPENING
    late = gate_weights[early:].reshape(OPENING * depth, columns)
    weights = lax.all_gather(late, "fsdp", axis=0)
    weights = weights.reshape(-1, 2, *weights.shape[1:])
    extra = jnp.pad(head_first, ((0, 0), (0, LANES))) + jnp.pad(
        head_second, ((0, HEAD_ROWS - head_second.shape[0]), (hidden, LANES - classes))
    )
    fsdp = lax.axis_index("fsdp")
    place = jnp.stack([fsdp // 8, fsdp // 2 % 4, fsdp % 2, lax.axis_index("dp")])
    pieces, stats, also = quarter_gather(
        gate_weights[:early].reshape(early * depth, columns), extra,
        stats.reshape(-1, LANES), (masks, b2, place, labels[:, None]), sizes, names, place,
    )
    masks, b2, place, labels = also
    stats = stats.reshape(2, width)
    *saved, state, low, turned, full = run_entry(
        place, features, stats, gain, bias, masks, pieces, early, total_rows
    )
    full = full.reshape(16, 2, early * depth, columns)
    grad_state, grad_scaled, top, sum1, sum2 = run_upper(
        place, masks, b1, b2, labels, weights, state, low, turned, pieces[:2], classes
    )
    top = lax.psum_scatter(top.reshape(-1, *top.shape[2:]), "fsdp", scatter_dimension=0)
    own_x, pass_x, grad_scaled, *sums = run_lower(
        place, masks, features, stats, saved, full, turned, grad_state, grad_scaled, total_rows
    )
    across = add(own_x, lax.ppermute(pass_x, names, pairs(sizes, 3, 1))).astype(BF16)
    across, sums = lax.optimization_barrier((across, sums))
    across = column_scatter(across)
    small = jnp.concatenate([sums[0].reshape(-1), sum1[0], sum2[0]])
    small = jnp.pad(small, (0, -small.size % 1024)).reshape(-1, LANES)
    small = everywhere_sum(small, sizes, names, (3, 2))
    small, across = lax.optimization_barrier((small, across))
    across = plane_scatter(across)
    small = everywhere_sum(small, sizes, names, (1, 0))
    small, across = lax.optimization_barrier((small, across))
    across = column_gather(across, sizes, names, place)
    small, top, across = lax.optimization_barrier((small, top, across))
    small = small.reshape(-1)
    cut = top.shape[0] // 32 * 16
    top = jnp.concatenate(
        [
            column_sum(top[:cut], sizes, names),
            column_sum(top[cut:], sizes, names, (3, 1)),
        ],
        0,
    )
    finished = [None] * sections
    order = list(range(sections))[::-1]
    for part, start, stop in ((top, 0, OPENING), (across, OPENING, sections)):
        for at, n in enumerate(order[start:stop]):
            finished[n] = part[at * depth : (at + 1) * depth]
    head_grad = top[OPENING * depth :]
    gate_grad = jnp.stack(finished, 0)
    head_first_grad = head_grad[:, :hidden]
    head_second_grad = head_grad[: head_second.shape[0], hidden : hidden + classes]

    sum_grad, sum_cross = small[:width], small[width : 2 * width]
    first_bias_grad = small[2 * width : 2 * width + hidden]
    second_bias_grad = small[2 * width + hidden : 2 * width + hidden + classes]
    normed, scale = normalise(total_rows, features, stats)
    features_grad = (
        scale * gain * (grad_scaled - sum_grad / total_rows - normed * (sum_cross / total_rows))
    )
    return (
        features_grad,
        sum_cross,
        sum_grad,
        gate_grad,
        head_first_grad,
        first_bias_grad,
        head_second_grad,
        second_bias_grad,
    )


def solution(mesh):
    placed = (
        P(("dp", "fsdp"), None),
        P(),
        P(),
        P(None, "fsdp", None),
        P(),
        P("fsdp", None),
        P(),
        P("fsdp", None),
        P(),
        P(("dp", "fsdp")),
    )
    sizes = (mesh.shape["dp"], 4, 4, mesh.shape["fsdp"] // 16)
    return jax.shard_map(
        functools.partial(on_device, sizes),
        mesh=mesh,
        in_specs=placed,
        out_specs=(
            P(("dp", "fsdp"), None),
            P(),
            P(),
            P(None, "fsdp", None),
            P("fsdp", None),
            P(),
            P("fsdp", None),
            P(),
        ),
        check_vma=False,
    )
```
